256 devices in a mesh: seq: 8 (over x, z_hi), head: 32 (over z_lo, y, core).
Axes of the slice: x: 4, y: 4, z: 8 (z_hi: 2, z_lo: 4; z = z_hi * 4 + z_lo), core: 2. Of those that a mesh axis runs over, the one named last changes fastest.
Arguments:
- tokens: bfloat16 [8192, 8192], P(('seq', 'head')), may hold values from -6 to 6
- in_x_weight: bfloat16 [8192, 10240], P(None, 'head'), may hold values from -0.0625 to 0.0625
- in_z_weight: bfloat16 [8192, 10240], P(None, 'head'), may hold values from -0.0625 to 0.0625
- in_bc_weight: bfloat16 [8192, 2048], P(None, 'head'), may hold values from -0.0625 to 0.0625
- in_dt_weight: bfloat16 [8192, 160], P(None, 'head'), may hold values from -0.0625 to 0.0625
- conv_x_weight: float32 [4, 10240], P(None, 'head'), may hold values from -3 to 3
- conv_bc_weight: float32 [4, 2048], P(None, 'head'), may hold values from -3 to 3
- dt_bias: float32 [160], P('head'), may hold values from -1 to 1
- a_log: float32 [160], P('head'), may hold values from -10 to -3.5
- skip_weight: float32 [160], P('head'), may hold values from 0.5 to 2
- norm_gain: float32 [10240], replicated, may hold values from 0.5 to 1.5
Outputs:
- mixed: bfloat16 [8192, 10240], P(('seq', 'head'))
The draws below stay inside these ranges and needn't reach their ends.
All inputs are finite; a program needn't handle non-finite values.
Results may differ from the reference program's by a relative error of at most 0.013.
Values may be sent and summed in bfloat16 or wider, within the bound.
A program may use at most 128 MiB of HBM per device.

```python
import jax
import jax.numpy as jnp
from jax import lax

D = 8192
HEADS = 160
HEAD_DIM = 64
STATE = 128
GROUPS = 8
NORM_GROUP = 2048
SPAN = 128
CONV = 4
DINNER = 10240
BCW = 2048
TOKENS = 8192


def block_levels(key, dims, shards, least, high):
    def one(axis_at, blocks):
        draws = jax.random.uniform(jax.random.fold_in(jax.random.fold_in(key, 6), axis_at), (blocks,), jnp.float32, least / len(shards), high / len(shards))
        return jnp.repeat(jnp.exp(draws), dims[axis_at] // blocks).reshape((-1,) + (1,) * (len(dims) - axis_at - 1))

    factor_of = one(*shards[0])
    for cut in shards[1:]:
        factor_of = factor_of * one(*cut)
    return factor_of


def noise(key, shape, scale, bound, split=(), dtype=jnp.bfloat16):
    result = scale * jax.random.normal(key, shape, jnp.float32)
    if split:
        result = result * block_levels(key, shape, split, -0.22, 0.18)
    return jnp.clip(result, -bound, bound).astype(dtype)


def setup_inputs(seed: int = 0) -> dict:
    streams_of = jax.random.split(jax.random.key(seed), 12)
    tokens = noise(streams_of[0], (TOKENS, D), 1.0, 6.0, ((0, 256),))
    in_x_weight = noise(streams_of[1], (D, DINNER), D ** -0.5, 0.0625, ((1, 32),))
    in_z_weight = noise(streams_of[2], (D, DINNER), D ** -0.5, 0.0625, ((1, 32),))
    in_bc_weight = noise(streams_of[3], (D, BCW), D ** -0.5, 0.0625, ((1, 32),))
    in_dt_weight = noise(streams_of[4], (D, HEADS), D ** -0.5, 0.0625, ((1, 32),))
    conv_x_weight = noise(streams_of[5], (CONV, DINNER), CONV ** -0.5, 3.0, ((1, 32),), jnp.float32)
    conv_bc_weight = noise(streams_of[6], (CONV, BCW), CONV ** -0.5, 3.0, ((1, 32),), jnp.float32)
    dt_bias = jnp.clip(jax.random.uniform(streams_of[7], (HEADS,), jnp.float32, -1.0, 1.0) * block_levels(streams_of[7], (HEADS,), ((0, 32),), -0.4, 0.0), -1.0, 1.0)
    a_log = jnp.clip(-10.0 + 6.5 * jax.random.uniform(streams_of[8], (HEADS,), jnp.float32) ** block_levels(streams_of[8], (HEADS,), ((0, 32),), -0.2, 0.2), -10.0, -3.5)
    skip_weight = jnp.clip(0.5 + 1.5 * jax.random.uniform(streams_of[9], (HEADS,), jnp.float32) ** block_levels(streams_of[9], (HEADS,), ((0, 32),), -0.2, 0.2), 0.5, 2.0)
    norm_gain = jnp.clip(1.0 + 0.1 * jax.random.normal(streams_of[10], (DINNER,), jnp.float32), 0.5, 1.5)
    return dict(tokens=tokens, in_x_weight=in_x_weight, in_z_weight=in_z_weight, in_bc_weight=in_bc_weight, in_dt_weight=in_dt_weight, conv_x_weight=conv_x_weight, conv_bc_weight=conv_bc_weight, dt_bias=dt_bias, a_log=a_log, skip_weight=skip_weight, norm_gain=norm_gain)


def causal_conv(pre, taps):
    width = pre.shape[1]
    padded = jnp.concatenate([jnp.zeros((CONV - 1, width), jnp.float32), pre.astype(jnp.float32)], axis=0)
    total = jnp.zeros((pre.shape[0], width), jnp.float32)
    for k in range(CONV):
        total = total + taps[k][None, :] * padded[k:k + pre.shape[0]]
    return jax.nn.silu(total).astype(jnp.bfloat16)

def reference(tokens, in_x_weight, in_z_weight, in_bc_weight, in_dt_weight, conv_x_weight, conv_bc_weight, dt_bias, a_log, skip_weight, norm_gain):
    high = lax.Precision.HIGHEST
    x_pre = jnp.dot(tokens, in_x_weight, preferred_element_type=jnp.float32).astype(jnp.bfloat16)
    z_gate = jnp.dot(tokens, in_z_weight, preferred_element_type=jnp.float32).astype(jnp.bfloat16)
    bc_pre = jnp.dot(tokens, in_bc_weight, preferred_element_type=jnp.float32).astype(jnp.bfloat16)
    dt_raw = jnp.dot(tokens, in_dt_weight, preferred_element_type=jnp.float32)
    x_conv = causal_conv(x_pre, conv_x_weight)
    bc_conv = causal_conv(bc_pre, conv_bc_weight)
    step_size = jax.nn.softplus(dt_raw + dt_bias[None, :])
    decay = -step_size * jnp.exp(a_log)[None, :]
    per_group = HEADS // GROUPS
    blocks = TOKENS // SPAN
    xs = x_conv.astype(jnp.float32).reshape(blocks, SPAN, HEADS, HEAD_DIM)
    bcs = bc_conv.astype(jnp.float32).reshape(blocks, SPAN, GROUPS, 2, STATE)
    decays = decay.reshape(blocks, SPAN, HEADS)
    steps_all = step_size.reshape(blocks, SPAN, HEADS)
    lower = jnp.arange(SPAN)[:, None] >= jnp.arange(SPAN)[None, :]

    def advance(state, inputs):
        xq, bcq, dq, sq = inputs
        bq = bcq[:, :, 0]
        cq = bcq[:, :, 1]
        cum = jnp.cumsum(dq, axis=0)
        diff = cum[:, None, :] - cum[None, :, :]
        lmat = jnp.exp(jnp.where(lower[:, :, None], diff, -jnp.inf))
        scores = jnp.einsum('ign,jgn->gij', cq, bq, precision=high)
        scores = jnp.repeat(scores, per_group, axis=0)
        mixing = scores * jnp.transpose(lmat, (2, 0, 1))
        inputs_u = xq * sq[:, :, None]
        y_in = jnp.einsum('hij,jhp->ihp', mixing, inputs_u, precision=high)
        ch = jnp.repeat(cq, per_group, axis=1)
        bh = jnp.repeat(bq, per_group, axis=1)
        y_st = jnp.einsum('ihn,hpn->ihp', ch, state, precision=high) * jnp.exp(cum)[:, :, None]
        tail = jnp.exp(cum[-1][None, :] - cum)
        fresh = jnp.einsum('jhp,jhn->hpn', inputs_u * tail[:, :, None], bh, precision=high)
        return (state * jnp.exp(cum[-1])[:, None, None] + fresh, y_in + y_st)
    start = jnp.zeros((HEADS, HEAD_DIM, STATE), jnp.float32)
    final, ys = lax.scan(advance, start, (xs, bcs, decays, steps_all))
    ys = ys.reshape(TOKENS, HEADS, HEAD_DIM) + skip_weight[None, :, None] * xs.reshape(TOKENS, HEADS, HEAD_DIM)
    y_ssd = ys.reshape(TOKENS, DINNER).astype(jnp.bfloat16)
    gated = y_ssd.astype(jnp.float32) * jax.nn.silu(z_gate.astype(jnp.float32))
    grouped = gated.reshape(TOKENS, DINNER // NORM_GROUP, NORM_GROUP)
    scale = lax.rsqrt(lax.optimization_barrier(jnp.mean(grouped * grouped, axis=2, keepdims=True)) + 1e-05)
    mixed = (grouped * scale).reshape(TOKENS, DINNER) * norm_gain[None, :]
    return mixed.astype(jnp.bfloat16)
```

```python
import jax
import jax.numpy as jnp
from jax import lax
from jax.experimental import pallas as pl
from jax.experimental.pallas import tpu as pltpu
from jax.sharding import PartitionSpec as P

MESH = pl.DeviceIdType.MESH
KC = 2048


def remote(src, dst, send, recv, head):
    return pltpu.make_async_remote_copy(
        src_ref=src, dst_ref=dst, send_sem=send, recv_sem=recv,
        device_id={"head": head}, device_id_type=MESH,
    )


def gather_kernel(tok, wx, wz, wbc, wdt, pre, dt,
                  buf, wt, res, zs, zr, ys, yr, ds, dr, lsem):
    h = lax.axis_index("head")
    z, y, c = h // 8, (h // 2) % 4, h % 2
    at = lambda zz, yy: zz * 8 + yy * 2 + c
    right, left, far = (y + 1) % 4, (y + 3) % 4, (y + 2) % 4
    sib = z * 8 + y * 2 + (1 - c)
    zz = jnp.where(z < 2, z, 3 - z)
    order = [jnp.where(z < 2, q, 3 - q) for q in (zz, 1 - zz, 2, 3)]
    width = wx.shape[0]
    nbc = wbc.shape[0]

    own = pltpu.make_async_copy(tok, buf.at[h], lsem.at[0])
    own.start()
    barrier = pltpu.get_barrier_semaphore()
    for peer in (at(z, right), at(z, left), sib):
        pl.semaphore_signal(barrier, inc=1, device_id={"head": peer}, device_id_type=MESH)

    @pl.when(z > 0)
    def _():
        pl.semaphore_signal(barrier, inc=1, device_id={"head": at(z - 1, y)}, device_id_type=MESH)

    @pl.when(z < 3)
    def _():
        pl.semaphore_signal(barrier, inc=1, device_id={"head": at(z + 1, y)}, device_id_type=MESH)

    pl.semaphore_wait(barrier, 3 + (z > 0).astype(jnp.int32) + (z < 3).astype(jnp.int32))
    own.wait()

    def zcopy(p, sign):
        slot = buf.at[at(p, y)]
        return remote(slot, slot, zs.at[p, (sign + 1) // 2], zr.at[p], at(z + sign, y))

    def zsend(p, sign, act):
        toward = (p <= z) if sign > 0 else (p >= z)
        room = (z < 3) if sign > 0 else (z > 0)

        @pl.when(jnp.logical_and(toward, room))
        def _():
            act(zcopy(p, sign))

    def ycopy(p, kind):
        if kind == 0:
            return remote(buf.at[at(p, y)], buf.at[at(p, y)], ys.at[p, 0], yr.at[p, 0], at(z, right))
        if kind == 1:
            return remote(buf.at[at(p, y)], buf.at[at(p, y)], ys.at[p, 1], yr.at[p, 1], at(z, left))
        if kind == 2:
            part = buf.at[at(p, left), pl.ds(0, 16)]
            return remote(part, part, ys.at[p, 2], yr.at[p, 2], at(z, right))
        part = buf.at[at(p, right), pl.ds(16, 16)]
        return remote(part, part, ys.at[p, 3], yr.at[p, 3], at(z, left))

    def ywait(p, kind):
        if kind == 0:
            part = buf.at[at(p, left)]
        elif kind == 1:
            part = buf.at[at(p, right)]
        elif kind == 2:
            part = buf.at[at(p, far), pl.ds(0, 16)]
        else:
            part = buf.at[at(p, far), pl.ds(16, 16)]
        remote(part, part, ys.at[p, kind], yr.at[p, kind], h).wait_recv()

    def dcopy(p, yy):
        slot = buf.at[at(p, yy)]
        return remote(slot, slot, ds.at[p, yy], dr.at[p, yy], sib)

    def dwait(p, yy):
        slot = buf.at[p * 8 + yy * 2 + 1 - c]
        remote(slot, slot, ds.at[p, yy], dr.at[p, yy], sib).wait_recv()

    def begin(p):
        ycopy(p, 0).start()
        ycopy(p, 1).start()
        dcopy(p, y).start()

    def near(p):
        ywait(p, 0)
        ycopy(p, 2).start()
        ywait(p, 1)
        ycopy(p, 3).start()
        dcopy(p, left).start()
        dcopy(p, right).start()

    def last(p):
        ywait(p, 2)
        ywait(p, 3)
        dcopy(p, far).start()

    def product(p):
        for yy in (y, left, right, far):
            dwait(p, yy)

        def chunk(k, _):
            ks = pl.ds(pl.multiple_of(k * KC, KC), KC)
            a = buf[pl.ds(p * 8, 8), :, ks].reshape(256, KC)
            part = lax.dot_general(wt[:, ks], a, (((1,), (1,)), ((), ())),
                                   preferred_element_type=jnp.float32)

            @pl.when(k == 0)
            def _():
                res[...] = part

            @pl.when(k > 0)
            def _():
                res[...] += part

            return 0

        lax.fori_loop(0, buf.shape[2] // KC, chunk, 0)
        span = pl.ds(pl.multiple_of(p * 256, 256), 256)
        n = pre.shape[0]
        pre[:, span] = res[0:n, :].astype(jnp.bfloat16)
        dt[:, span] = res[n : n + 16, :]

    zsend(order[0], 1, lambda d: d.start())
    zsend(order[0], -1, lambda d: d.start())
    begin(order[0])
    loads = [
        pltpu.make_async_copy(wx, wt.at[pl.ds(0, width)], lsem.at[1]),
        pltpu.make_async_copy(wz, wt.at[pl.ds(width, width)], lsem.at[2]),
        pltpu.make_async_copy(wbc, wt.at[pl.ds(2 * width, nbc)], lsem.at[3]),
    ]
    for load in loads:
        load.start()
    n = 2 * width + nbc
    wt[n : n + 16, :] = jnp.concatenate(
        [wdt[...].astype(jnp.float32), jnp.zeros((16 - wdt.shape[0], wt.shape[1]), jnp.float32)], axis=0
    ).astype(jnp.bfloat16)
    for load in loads:
        load.wait()

    for j in range(1, 4):
        p = order[j]
        slot = buf.at[at(p, y)]
        remote(slot, slot, zs.at[p, 0], zr.at[p], h).wait_recv()
        zsend(p, 1, lambda d: d.start())
        zsend(p, -1, lambda d: d.start())
        begin(p)
        near(order[j - 1])
        if j >= 2:
            last(order[j - 2])
        if j >= 3:
            product(order[j - 3])
    near(order[3])
    last(order[2])
    product(order[1])
    product(order[2])
    last(order[3])
    product(order[3])
    for j in range(4):
        p = order[j]
        zsend(p, 1, lambda d: d.wait_send())
        zsend(p, -1, lambda d: d.wait_send())
        for kind in range(4):
            ycopy(p, kind).wait_send()
        for yy in range(4):
            dcopy(p, yy).wait_send()


def gather_call(tok, wx, wz, wbc, wdt):
    d = tok.shape[1]
    n = 2 * wx.shape[0] + wbc.shape[0]
    anyspec = pl.BlockSpec(memory_space=pl.ANY)
    vm = pl.BlockSpec(memory_space=pltpu.VMEM)
    dma = pltpu.SemaphoreType.DMA
    return pl.pallas_call(
        gather_kernel,
        out_shape=(jax.ShapeDtypeStruct((n, 1024), jnp.bfloat16),
                   jax.ShapeDtypeStruct((16, 1024), jnp.float32)),
        in_specs=[anyspec] * 4 + [vm],
        out_specs=(vm, vm),
        scratch_shapes=[
            pltpu.VMEM((32, 32, d), jnp.bfloat16),
            pltpu.VMEM((n + 16, d), jnp.bfloat16),
            pltpu.VMEM((n + 16, 256), jnp.float32),
            dma((4, 2)), dma((4,)), dma((4, 4)), dma((4, 4)), dma((4, 4)), dma((4, 4)), dma((4,)),
        ],
        compiler_params=pltpu.CompilerParams(collective_id=0, has_side_effects=True,
                                             vmem_limit_bytes=60 * 2**20),
        name="gather_project",
    )(tok, wx, wz, wbc, wdt)


F32 = jnp.float32
BF16 = jnp.bfloat16
NT = (((1,), (1,)), ((), ()))
TN = (((0,), (0,)), ((), ()))


def rcopy(src, dst, send, recv, **device):
    return pltpu.make_async_remote_copy(
        src_ref=src, dst_ref=dst, send_sem=send, recv_sem=recv,
        device_id=device, device_id_type=MESH,
    )


def silu(v):
    return v / (1.0 + jnp.exp(-v))


def mix_kernel(pre, dt, cx, cbc, bias, alog, skip, gain, out,
               halo_out, halo_in, hpad, xc, bcf, step, cums, cumt, yin, sstart, sfin, tfin,
               st_in, tot_in, inc, sb, rbuf, asm,
               hs, hr, bs, br, ss, sr, ts, tr, as_, ar):
    h = lax.axis_index("head")
    s = lax.axis_index("seq")
    heads, W = 5, 320
    ZB, BB = W, 2 * W
    nseq = 8

    barrier = pltpu.get_barrier_semaphore()

    def greet(k, _):
        pl.semaphore_signal(barrier, inc=1, device_id={"head": (h + k) % 32}, device_id_type=MESH)
        return 0

    lax.fori_loop(1, 32, greet, 0)

    def greet_seq(k, _):
        pl.semaphore_signal(barrier, inc=1, device_id={"seq": (s + k) % nseq}, device_id_type=MESH)
        return 0

    lax.fori_loop(1, nseq, greet_seq, 0)
    pl.semaphore_wait(barrier, 31 + nseq - 1)

    pick = (lax.broadcasted_iota(jnp.int32, (16, 128), 1)
            == lax.broadcasted_iota(jnp.int32, (16, 128), 0) + 112).astype(BF16)
    halo_out[:, 0:W] = lax.dot_general(pick, pre[0:W, 896:1024], NT, preferred_element_type=F32).astype(BF16)
    halo_out[:, 384:448] = lax.dot_general(pick, pre[BB:BB + 64, 896:1024], NT, preferred_element_type=F32).astype(BF16)

    @pl.when(s < nseq - 1)
    def _():
        rcopy(halo_out, halo_in, hs, hr, seq=s + 1).start()

    row = lax.broadcasted_iota(jnp.int32, (8, 128), 0)
    bias_col = jnp.zeros((8, 128), F32)
    rate_col = jnp.zeros((8, 128), F32)
    for k in range(heads):
        bias_col = jnp.where(row == k, bias[k], bias_col)
        rate_col = jnp.where(row == k, alog[k], rate_col)
    rate_col = jnp.exp(rate_col)
    upper = (lax.broadcasted_iota(jnp.int32, (128, 128), 0)
             <= lax.broadcasted_iota(jnp.int32, (128, 128), 1))
    parts = []
    for b in range(8):
        v = dt[0:8, b * 128:(b + 1) * 128] + bias_col
        v = jnp.maximum(v, 0.0) + jnp.log1p(jnp.exp(-jnp.abs(v)))
        step[b * 8:(b + 1) * 8, :] = v
        parts.append(-v * rate_col)
    dec = jnp.concatenate(parts, axis=0)
    cum = jnp.dot(dec, upper.astype(F32), preferred_element_type=F32, precision=lax.Precision.HIGHEST)
    cums[...] = cum
    tot = jnp.broadcast_to(cum[:, 127:128], (64, 128))
    weight = step[...] * jnp.exp(tot - cum)
    cumt[...] = (cum - jnp.log(step[...])).T

    @pl.when(s == 0)
    def _():
        hpad[...] = jnp.zeros_like(hpad)

    @pl.when(s > 0)
    def _():
        rcopy(halo_out, halo_in, hs, hr, seq=s).wait_recv()
        hpad[0:W, :] = lax.dot_general(halo_in[:, 0:W], pick, TN, preferred_element_type=F32)
        hpad[W:W + 64, :] = lax.dot_general(halo_in[:, 384:448], pick, TN, preferred_element_type=F32)

    lane = lax.broadcasted_iota(jnp.int32, (64, 128), 1)
    tapx = jnp.concatenate([cx[...], jnp.zeros((4, W), F32)], axis=0).T
    tapb = jnp.concatenate([cbc[...], jnp.zeros((4, 64), F32)], axis=0).T

    def conv(r0, taps, hrow, dst, drow):
        prev = hpad[hrow:hrow + 64, :]
        for b in range(8):
            cur = pre[r0:r0 + 64, b * 128:(b + 1) * 128].astype(F32)
            total = taps[:, 3:4] * cur
            for k in range(1, 4):
                moved = pltpu.roll(jnp.where(lane >= 128 - k, prev, cur), k, 1)
                total = total + taps[:, 3 - k:4 - k] * moved
            dst[pl.ds(drow, 64), b * 128:(b + 1) * 128] = silu(total).astype(BF16)
            prev = cur

    mine = pl.multiple_of((h % 4) * 64, 64)
    conv(BB, tapb, W, bcf, mine)
    base = (h // 4) * 4
    slot = bcf.at[pl.ds(mine, 64)]
    for k in range(1, 4):
        rcopy(slot, slot, bs.at[k], br.at[h % 4], head=base + (h + k) % 4).start()
    for k in range(heads):
        conv(k * 64, tapx[k * 64:(k + 1) * 64], k * 64, xc, k * 64)
    for k in range(1, 4):
        q = (h + k) % 4
        other = bcf.at[pl.ds(pl.multiple_of(q * 64, 64), 64)]
        rcopy(other, other, bs.at[k], br.at[q], head=h).wait_recv()

    def rows(v, r):
        return jnp.concatenate(
            [jnp.broadcast_to(v[r + k:r + k + 1, :], (64, 128)) for k in range(heads)], axis=0)

    state = jnp.zeros((W, 128), F32)
    total = jnp.zeros((8, 128), F32)
    for b in range(8):
        cols = slice(b * 128, (b + 1) * 128)
        sstart[b] = state
        xw = (xc[:, cols].astype(F32) * rows(weight, b * 8)).astype(BF16)
        fresh = lax.dot_general(xw, bcf[0:128, cols], NT, preferred_element_type=F32)
        tb = tot[b * 8:(b + 1) * 8, :]
        state = state * rows(jnp.exp(tb), 0) + fresh
        total = total + tb
    sfin[...] = state.astype(BF16)
    tfin[...] = total
    for t in range(1, nseq):
        @pl.when(s + t < nseq)
        def _():
            rcopy(sfin, st_in.at[s], ss.at[t], sr.at[s], seq=s + t).start()
            rcopy(tfin, tot_in.at[s], ts.at[t], tr.at[s], seq=s + t).start()

    for b in range(8):
        cols = slice(b * 128, (b + 1) * 128)
        scores = lax.dot_general(bcf[0:128, cols], bcf[128:256, cols], TN, preferred_element_type=F32)
        scores = jnp.where(upper, scores, 0.0)
        for k in range(heads):
            r = b * 8 + k
            diff = cums[r:r + 1, :] - cumt[:, r:r + 1]
            mixing = jnp.exp(jnp.where(upper, diff, -jnp.inf)) * scores
            yin[k * 64:(k + 1) * 64, cols] = jnp.dot(
                xc[k * 64:(k + 1) * 64, cols], mixing.astype(BF16), preferred_element_type=F32)

    inc[...] = jnp.zeros_like(inc)
    for q in range(nseq - 1):
        @pl.when(q < s)
        def _():
            rcopy(sfin, st_in.at[q], ss.at[0], sr.at[q], seq=s).wait_recv()
            rcopy(tfin, tot_in.at[q], ts.at[0], tr.at[q], seq=s).wait_recv()
            inc[...] = inc[...] * rows(jnp.exp(tot_in[q]), 0) + st_in[q].astype(F32)

    skips = jnp.concatenate([jnp.full((64, 128), skip[k], F32) for k in range(heads)], axis=0)
    offset = jnp.zeros((8, 128), F32)
    for b in range(8):
        cols = slice(b * 128, (b + 1) * 128)
        st = (sstart[b] + inc[...] * rows(jnp.exp(offset), 0)).astype(BF16)
        yst = jnp.dot(st, bcf[128:256, cols], preferred_element_type=F32)
        y = yin[:, cols] + yst * rows(jnp.exp(cums[b * 8:(b + 1) * 8, :]), 0) + skips * xc[:, cols].astype(F32)
        y = y.astype(BF16).astype(F32)
        g = y * silu(pre[ZB:ZB + W, cols].astype(F32))
        gt = g.T
        for i in range(4):
            sb[4 * b + i, :, 0:W] = gt[32 * i:32 * i + 16, :].astype(BF16)
            sb[4 * b + i, :, W:2 * W] = gt[32 * i + 16:32 * i + 32, :].astype(BF16)
        offset = offset + tot[b * 8:(b + 1) * 8, :]

    def scatter(k, _):
        dst = (h + k) % 32
        rcopy(sb.at[dst], rbuf.at[h], as_.at[dst], ar.at[h], head=dst).start()
        return 0

    lax.fori_loop(1, 32, scatter, 0)
    rbuf[h] = sb[h]

    def collect(k, _):
        src = (h + k) % 32
        rcopy(sb.at[src], rbuf.at[src], as_.at[src], ar.at[src], head=h).wait_recv()
        return 0

    lax.fori_loop(1, 32, collect, 0)

    for q in range(32):
        asm[0:16, q * W:(q + 1) * W] = rbuf[q, :, 0:W]
        asm[16:32, q * W:(q + 1) * W] = rbuf[q, :, W:2 * W]
    for g in range(5):
        v = asm[:, g * 2048:(g + 1) * 2048].astype(F32)
        scale = lax.rsqrt(jnp.mean(v * v, axis=1, keepdims=True) + 1e-5)
        for k in range(16):
            c0 = g * 16 + k
            out[:, c0 * 128:(c0 + 1) * 128] = (
                v[:, k * 128:(k + 1) * 128] * scale * gain[c0:c0 + 1, :]).astype(BF16)

    @pl.when(s < nseq - 1)
    def _():
        rcopy(halo_out, halo_in, hs, hr, seq=s + 1).wait_send()

    for k in range(1, 4):
        rcopy(slot, slot, bs.at[k], br.at[h % 4], head=h).wait_send()
    for t in range(1, nseq):
        @pl.when(s + t < nseq)
        def _():
            rcopy(sfin, st_in.at[s], ss.at[t], sr.at[s], seq=s).wait_send()
            rcopy(tfin, tot_in.at[s], ts.at[t], tr.at[s], seq=s).wait_send()

    def sent(k, _):
        dst = (h + k) % 32
        rcopy(sb.at[dst], rbuf.at[h], as_.at[dst], ar.at[h], head=h).wait_send()
        return 0

    lax.fori_loop(1, 32, sent, 0)


def mix_scratch():
    dma = pltpu.SemaphoreType.DMA
    vm = pltpu.VMEM
    return [
        vm((16, 512), BF16), vm((16, 512), BF16), vm((384, 128), F32),
        vm((320, 1024), BF16), vm((256, 1024), BF16), vm((64, 128), F32), vm((64, 128), F32),
        vm((128, 64), F32), vm((320, 1024), F32), vm((8, 320, 128), F32),
        vm((320, 128), BF16), vm((8, 128), F32),
        vm((8, 320, 128), BF16), vm((8, 8, 128), F32), vm((320, 128), F32),
        vm((32, 16, 640), BF16), vm((32, 16, 640), BF16), vm((32, 10240), BF16),
        dma, dma, dma((4,)), dma((4,)), dma((8,)), dma((8,)), dma((8,)), dma((8,)),
        dma((32,)), dma((32,)),
    ]


def mix_call(pre, dt, cx, cbc, bias, alog, skip, gain):
    vm = pl.BlockSpec(memory_space=pltpu.VMEM)
    sm = pl.BlockSpec(memory_space=pltpu.SMEM)
    return pl.pallas_call(
        mix_kernel,
        out_shape=jax.ShapeDtypeStruct((32, 10240), BF16),
        in_specs=[vm] * 4 + [sm] * 3 + [vm],
        out_specs=vm,
        scratch_shapes=mix_scratch(),
        compiler_params=pltpu.CompilerParams(collective_id=1, has_side_effects=True,
                                             vmem_limit_bytes=60 * 2**20),
        name="mix",
    )(pre, dt, cx, cbc, bias, alog, skip, gain.reshape(80, 128))


def shards(tokens, wx, wz, wbc, wdt, cx, cbc, bias, alog, skip, gain):
    pre, dt = gather_call(tokens, wx.T, wz.T, wbc.T, wdt.T)
    return mix_call(pre, dt, cx, cbc, bias, alog, skip, gain)


def solution(mesh):
    cols = P(None, "head")
    placed = (P(("seq", "head"), None), cols, cols, cols, cols, cols, cols,
              P("head"), P("head"), P("head"), P())
    return jax.shard_map(
        shards, mesh=mesh, in_specs=placed, out_specs=P(("seq", "head"), None), check_vma=False
    )
```

```python
import jax
import jax.numpy as jnp
from jax import lax
from jax.experimental import pallas as pl
from jax.experimental.pallas import tpu as pltpu
from jax.sharding import PartitionSpec as P

MESH = pl.DeviceIdType.MESH
F32 = jnp.float32
BF16 = jnp.bfloat16
NT = (((1,), (1,)), ((), ()))
TN = (((0,), (0,)), ((), ()))
KC = 4096
EARLY = 1536
HEADS = 5
W = 320
BB = 2 * W
FIRST = W + 80
NSEQ = 8


def rcopy(src, dst, send, recv, **device):
    return pltpu.make_async_remote_copy(
        src_ref=src, dst_ref=dst, send_sem=send, recv_sem=recv,
        device_id=device, device_id_type=MESH,
    )


def silu(v):
    return v / (1.0 + jnp.exp(-v))


def kernel(tok, wx, wz, wbc, wdt, cx, cbc, bias, alog, skip, gain, out,
           buf, wt, res, pre, dt, bcp, bcf, halo_x, halo_b, in_x, in_b, hpad, taps, xc,
           step, cums, cumt, yin, sstart, sfin, tfin, st_in, tot_in, inc, sb, rbuf, asm,
           lsem, zs, zr, es, er, ys, yr, ds, dr, fs, fr,
           bs, br, cs, cr, hxs, hxr, hbs, hbr, ss, sr, ts, tr, as_, ar):
    h = lax.axis_index("head")
    s = lax.axis_index("seq")
    z, y, c = h // 8, (h // 2) % 4, h % 2
    right, left, far = (y + 1) % 4, (y + 3) % 4, (y + 2) % 4
    sib = h + 1 - 2 * c
    across = h + 2 - 4 * (y % 2)
    base = (h // 4) * 4
    quarter = h % 4
    zz = jnp.where(z < 2, z, 3 - z)
    order = [jnp.where(z < 2, q, 3 - q) for q in (zz, 1 - zz, 2, 3)]

    def at(p, yy):
        return p * 8 + yy * 2 + c

    own = pltpu.make_async_copy(tok, buf.at[h], lsem.at[0])
    own.start()
    loads = [
        pltpu.make_async_copy(wx, wt.at[pl.ds(0, W)], lsem.at[1]),
        pltpu.make_async_copy(wz, wt.at[pl.ds(FIRST, W)], lsem.at[2]),
        pltpu.make_async_copy(wbc, wt.at[pl.ds(W, 64)], lsem.at[3]),
    ]
    barrier = pltpu.get_barrier_semaphore()

    def greet(k, _):
        pl.semaphore_signal(barrier, inc=1, device_id={"head": (h + k) % 32}, device_id_type=MESH)
        return 0

    def greet_seq(k, _):
        pl.semaphore_signal(barrier, inc=1, device_id={"seq": (s + k) % NSEQ}, device_id_type=MESH)
        return 0

    lax.fori_loop(1, 32, greet, 0)
    lax.fori_loop(1, NSEQ, greet_seq, 0)

    @pl.when(s > 0)
    def _():
        for k in range(1, 4):
            pl.semaphore_signal(barrier, inc=1, device_id={"seq": s - 1, "head": base + (h + k) % 4},
                                device_id_type=MESH)

    pl.semaphore_wait(barrier, 31 + NSEQ - 1 + 3 * (s < NSEQ - 1).astype(jnp.int32))
    own.wait()

    early = pl.ds(0, EARLY)
    late = pl.ds(EARLY, buf.shape[2] - EARLY)

    def along(p, sign, act):
        toward = (p <= z) if sign > 0 else (p >= z)
        room = (z < 3) if sign > 0 else (z > 0)

        @pl.when(jnp.logical_and(toward, room))
        def _():
            slot = buf.at[at(p, y)]
            act(rcopy(slot, slot, zs.at[p, (sign + 1) // 2], zr.at[p], head=at(z + sign, y)))

    def along_early(p, yy, sign, act):
        toward = (p <= z) if sign > 0 else (p >= z)
        room = (z < 3) if sign > 0 else (z > 0)

        @pl.when(jnp.logical_and(toward, room))
        def _():
            slot = buf.at[at(p, yy), :, early]
            act(rcopy(slot, slot, es.at[p, yy, (sign + 1) // 2], er.at[p, yy], head=at(z + sign, y)))

    def both(move, *where):
        move(*where, 1, lambda d: d.start())
        move(*where, -1, lambda d: d.start())

    def ring(p, kind, own_plane):
        cols = pl.ds(0, buf.shape[2]) if own_plane else late
        yy, rows, to = (
            (y, pl.ds(0, 32), right), (y, pl.ds(0, 32), left),
            (left, pl.ds(0, 16), right), (right, pl.ds(16, 16), left),
        )[kind]
        part = buf.at[at(p, yy), rows, cols]
        return rcopy(part, part, ys.at[p, kind], yr.at[p, kind], head=at(z, to))

    def ring_wait(p, kind, own_plane):
        cols = pl.ds(0, buf.shape[2]) if own_plane else late
        yy, rows = ((left, pl.ds(0, 32)), (right, pl.ds(0, 32)),
                    (far, pl.ds(0, 16)), (far, pl.ds(16, 16)))[kind]
        part = buf.at[at(p, yy), rows, cols]
        rcopy(part, part, ys.at[p, kind], yr.at[p, kind], head=h).wait_recv()

    def twin(p, yy, whole):
        slot = buf.at[at(p, yy)] if whole else buf.at[at(p, yy), :, late]
        return rcopy(slot, slot, ds.at[p, yy], dr.at[p, yy], head=sib)

    def twin_wait(p, yy, whole):
        slot = buf.at[p * 8 + yy * 2 + 1 - c]
        slot = slot if whole else slot.at[:, late]
        rcopy(slot, slot, ds.at[p, yy], dr.at[p, yy], head=h).wait_recv()

    def twin_early(p, yy):
        slot = buf.at[at(p, yy), :, early]
        return rcopy(slot, slot, fs.at[p, yy], fr.at[p, yy], head=sib)

    def twin_early_wait(p, yy):
        slot = buf.at[p * 8 + yy * 2 + 1 - c, :, early]
        rcopy(slot, slot, fs.at[p, yy], fr.at[p, yy], head=h).wait_recv()

    def begin(p, own_plane):
        ring(p, 0, own_plane).start()
        ring(p, 1, own_plane).start()
        twin(p, y, True).start()

    def arrive(p):
        slot = buf.at[at(p, y)]
        rcopy(slot, slot, zs.at[p, 0], zr.at[p], head=h).wait_recv()
        both(along, p)
        begin(p, False)

    def arrive_early(p):
        for yy in (left, right, far):
            slot = buf.at[at(p, yy), :, early]
            rcopy(slot, slot, es.at[p, yy, 0], er.at[p, yy], head=h).wait_recv()
            both(along_early, p, yy)
            twin_early(p, yy).start()

    def near(p, own_plane):
        ring_wait(p, 0, own_plane)
        ring(p, 2, own_plane).start()
        ring_wait(p, 1, own_plane)
        ring(p, 3, own_plane).start()
        for yy in (left, right):
            twin(p, yy, own_plane).start()
            if own_plane:
                both(along_early, p, yy)

    def last(p, own_plane):
        ring_wait(p, 2, own_plane)
        ring_wait(p, 3, own_plane)
        twin(p, far, own_plane).start()
        if own_plane:
            both(along_early, p, far)

    def complete(p, own_plane):
        twin_wait(p, y, True)
        for yy in (left, right, far):
            twin_wait(p, yy, own_plane)
            if not own_plane:
                twin_early_wait(p, yy)

    def product(p, r0, n):
        def chunk(k, _):
            ks = pl.ds(pl.multiple_of(k * KC, KC), KC)
            a = buf[pl.ds(p * 8, 8), :, ks].reshape(256, KC)
            part = lax.dot_general(wt[r0:r0 + n, ks], a, NT, preferred_element_type=F32)

            @pl.when(k == 0)
            def _():
                res[r0:r0 + n] = part

            @pl.when(k > 0)
            def _():
                res[r0:r0 + n] += part

            return 0

        lax.fori_loop(0, buf.shape[2] // KC, chunk, 0)

    def span_of(p):
        return pl.ds(pl.multiple_of(p * 256, 256), 256)

    def quarter_rows(q):
        return pl.ds(pl.multiple_of(q * 64, 64), 64)

    q_sib = quarter + 1 - 2 * c
    q_across = quarter + 2 - 4 * (y % 2)
    q_other = q_across + 1 - 2 * c

    def share_copy(p, kind):
        q = (quarter, quarter, q_across)[kind]
        part = bcp.at[quarter_rows(q), span_of(p)]
        return rcopy(part, part, bs.at[p, kind], br.at[p, kind], head=(sib, across, sib)[kind])

    def share_wait(p, kind):
        q = (q_sib, q_across, q_other)[kind]
        part = bcp.at[quarter_rows(q), span_of(p)]
        rcopy(part, part, bs.at[p, kind], br.at[p, kind], head=h).wait_recv()

    def store_bc(p):
        span = span_of(p)
        bcp[quarter_rows(quarter), span] = res[W:W + 64].astype(BF16)
        dt[:, span] = res[W + 64:FIRST]
        share_copy(p, 0).start()
        share_copy(p, 1).start()

    def pass_bc(p):
        share_wait(p, 1)
        share_copy(p, 2).start()

    def store_x(p):
        pre[0:W, span_of(p)] = res[0:W].astype(BF16)

    def store_z(p):
        pre[W:BB, span_of(p)] = res[FIRST:FIRST + W].astype(BF16)

    pick = (lax.broadcasted_iota(jnp.int32, (16, 128), 1)
            == lax.broadcasted_iota(jnp.int32, (16, 128), 0) + 112).astype(BF16)

    def halo_copies():
        yield rcopy(halo_x, in_x, hxs, hxr, seq=s + 1)
        for k in range(4):
            yield rcopy(halo_b, in_b.at[quarter], hbs.at[k], hbr.at[quarter], seq=s + 1, head=base + k)

    def send_halo(p):
        @pl.when(jnp.logical_and(p == 3, s < NSEQ - 1))
        def _():
            tail = pl.ds(896, 128)
            halo_x[:, 0:W] = lax.dot_general(pick, pre[0:W, tail], NT, preferred_element_type=F32).astype(BF16)
            halo_b[:, 0:64] = lax.dot_general(
                pick, bcp[quarter_rows(quarter), tail], NT, preferred_element_type=F32).astype(BF16)
            for copy in halo_copies():
                copy.start()

    def project(p, own_plane):
        complete(p, own_plane)
        product(p, 0, FIRST)
        store_bc(p)
        store_x(p)
        send_halo(p)

    def gates(p):
        product(p, FIRST, W)
        store_z(p)

    def taps_copy(k):
        slot = taps.at[quarter]
        return rcopy(slot, slot, cs.at[k], cr.at[quarter], head=base + (h + k + 1) % 4)

    def taps_wait(k):
        q = (h + k + 1) % 4
        rcopy(taps.at[q], taps.at[q], cs.at[k], cr.at[q], head=h).wait_recv()

    both(along, order[0])
    begin(order[0], True)
    for load in loads:
        load.start()
    taps[quarter, 0:4, 0:64] = cbc[...]
    for k in range(3):
        taps_copy(k).start()
    wt[W + 64:FIRST, :] = jnp.concatenate(
        [wdt[...].astype(F32), jnp.zeros((16 - HEADS, wt.shape[1]), F32)], axis=0).astype(BF16)
    halo_x[...] = jnp.zeros_like(halo_x)
    halo_b[...] = jnp.zeros_like(halo_b)
    for load in loads:
        load.wait()

    arrive(order[1])
    near(order[0], True)
    arrive(order[2])
    last(order[0], True)
    near(order[1], False)
    arrive(order[3])
    project(order[0], True)
    arrive_early(order[2])
    arrive_early(order[1])
    near(order[2], False)
    last(order[1], False)
    gates(order[0])
    arrive_early(order[3])
    near(order[3], False)
    project(order[1], False)
    pass_bc(order[0])
    last(order[2], False)
    gates(order[1])
    project(order[2], False)
    pass_bc(order[1])
    last(order[3], False)
    gates(order[2])
    pass_bc(order[2])
    project(order[3], False)
    pass_bc(order[3])

    row = lax.broadcasted_iota(jnp.int32, (8, 128), 0)
    bias_col = jnp.zeros((8, 128), F32)
    rate_col = jnp.zeros((8, 128), F32)
    for k in range(HEADS):
        bias_col = jnp.where(row == k, bias[k], bias_col)
        rate_col = jnp.where(row == k, alog[k], rate_col)
    rate_col = jnp.exp(rate_col)
    upper = (lax.broadcasted_iota(jnp.int32, (128, 128), 0)
             <= lax.broadcasted_iota(jnp.int32, (128, 128), 1))
    parts = []
    for b in range(8):
        v = dt[0:8, b * 128:(b + 1) * 128] + bias_col
        v = jnp.maximum(v, 0.0) + jnp.log1p(jnp.exp(-jnp.abs(v)))
        step[b * 8:(b + 1) * 8, :] = v
        parts.append(-v * rate_col)
    dec = jnp.concatenate(parts, axis=0)
    cum = jnp.dot(dec, upper.astype(F32), preferred_element_type=F32, precision=lax.Precision.HIGHEST)
    cums[...] = cum
    tot = jnp.broadcast_to(cum[:, 127:128], (64, 128))
    weight = step[...] * jnp.exp(tot - cum)
    cumt[...] = (cum - jnp.log(step[...])).T

    lane = lax.broadcasted_iota(jnp.int32, (64, 128), 1)
    tapx = jnp.concatenate([cx[...], jnp.zeros((4, W), F32)], axis=0).T

    def conv(src, r0, taps, hrow, dst, first, count):
        prev = hpad[hrow:hrow + 64, :] if first == 0 else src[r0:r0 + 64, (first - 1) * 128:first * 128].astype(F32)
        for b in range(first, first + count):
            cur = src[r0:r0 + 64, b * 128:(b + 1) * 128].astype(F32)
            total = taps[:, 3:4] * cur
            for k in range(1, 4):
                moved = pltpu.roll(jnp.where(lane >= 128 - k, prev, cur), k, 1)
                total = total + taps[:, 3 - k:4 - k] * moved
            dst[r0:r0 + 64, b * 128:(b + 1) * 128] = silu(total).astype(BF16)
            prev = cur

    for k in range(HEADS):
        conv(pre, k * 64, tapx[k * 64:(k + 1) * 64], 0, xc, 1, 7)
    for p in range(4):
        share_wait(p, 0)
        share_wait(p, 2)
    for k in range(3):
        taps_wait(k)
    tapb = [taps[q].T[0:64] for q in range(4)]
    for q in range(4):
        conv(bcp, q * 64, tapb[q], 0, bcf, 1, 7)

    @pl.when(s == 0)
    def _():
        hpad[...] = jnp.zeros_like(hpad)

    @pl.when(s > 0)
    def _():
        rcopy(halo_x, in_x, hxs, hxr, seq=s).wait_recv()
        hpad[0:W, :] = lax.dot_general(in_x[:, 0:W], pick, TN, preferred_element_type=F32)
        for q in range(4):
            rcopy(halo_b, in_b.at[q], hbs.at[0], hbr.at[q], seq=s).wait_recv()
            hpad[W + q * 64:W + q * 64 + 64, :] = lax.dot_general(
                in_b[q, :, 0:64], pick, TN, preferred_element_type=F32)

    for k in range(HEADS):
        conv(pre, k * 64, tapx[k * 64:(k + 1) * 64], k * 64, xc, 0, 1)
    for q in range(4):
        conv(bcp, q * 64, tapb[q], W + q * 64, bcf, 0, 1)

    def rows(v, r):
        return jnp.concatenate(
            [jnp.broadcast_to(v[r + k:r + k + 1, :], (64, 128)) for k in range(HEADS)], axis=0)

    state = jnp.zeros((W, 128), F32)
    total = jnp.zeros((8, 128), F32)
    for b in range(8):
        cols = slice(b * 128, (b + 1) * 128)
        sstart[b] = state
        xw = (xc[:, cols].astype(F32) * rows(weight, b * 8)).astype(BF16)
        fresh = lax.dot_general(xw, bcf[0:128, cols], NT, preferred_element_type=F32)
        tb = tot[b * 8:(b + 1) * 8, :]
        state = state * rows(jnp.exp(tb), 0) + fresh
        total = total + tb
    sfin[...] = state.astype(BF16)
    tfin[...] = total
    for t in range(1, NSEQ):
        @pl.when(s + t < NSEQ)
        def _():
            rcopy(sfin, st_in.at[s], ss.at[t], sr.at[s], seq=s + t).start()
            rcopy(tfin, tot_in.at[s], ts.at[t], tr.at[s], seq=s + t).start()

    gates(order[3])
    for b in range(8):
        cols = slice(b * 128, (b + 1) * 128)
        scores = lax.dot_general(bcf[0:128, cols], bcf[128:256, cols], TN, preferred_element_type=F32)
        scores = jnp.where(upper, scores, 0.0)
        for k in range(HEADS):
            r = b * 8 + k
            diff = cums[r:r + 1, :] - cumt[:, r:r + 1]
            mixing = jnp.exp(jnp.where(upper, diff, -jnp.inf)) * scores
            yin[k * 64:(k + 1) * 64, cols] = jnp.dot(
                xc[k * 64:(k + 1) * 64, cols], mixing.astype(BF16), preferred_element_type=F32)

    inc[...] = jnp.zeros_like(inc)
    for q in range(NSEQ - 1):
        @pl.when(q < s)
        def _():
            rcopy(sfin, st_in.at[q], ss.at[0], sr.at[q], seq=s).wait_recv()
            rcopy(tfin, tot_in.at[q], ts.at[0], tr.at[q], seq=s).wait_recv()
            inc[...] = inc[...] * rows(jnp.exp(tot_in[q]), 0) + st_in[q].astype(F32)

    skips = jnp.concatenate([jnp.full((64, 128), skip[k], F32) for k in range(HEADS)], axis=0)
    offset = jnp.zeros((8, 128), F32)
    for b in range(8):
        cols = slice(b * 128, (b + 1) * 128)
        st = (sstart[b] + inc[...] * rows(jnp.exp(offset), 0)).astype(BF16)
        yst = jnp.dot(st, bcf[128:256, cols], preferred_element_type=F32)
        yv = yin[:, cols] + yst * rows(jnp.exp(cums[b * 8:(b + 1) * 8, :]), 0) + skips * xc[:, cols].astype(F32)
        yv = yv.astype(BF16).astype(F32)
        g = (yv * silu(pre[W:BB, cols].astype(F32))).T
        for i in range(4):
            sb[4 * b + i, :, 0:W] = g[32 * i:32 * i + 16, :].astype(BF16)
            sb[4 * b + i, :, W:BB] = g[32 * i + 16:32 * i + 32, :].astype(BF16)
        offset = offset + tot[b * 8:(b + 1) * 8, :]

    def scatter(k, _):
        dst = (h + 16 + k) % 32

        @pl.when(k != 16)
        def _():
            rcopy(sb.at[dst], rbuf.at[h], as_.at[dst], ar.at[h], head=dst).start()

        return 0

    lax.fori_loop(0, 32, scatter, 0)
    rbuf[h] = sb[h]

    def collect(k, _):
        src = (h + k) % 32
        rcopy(sb.at[src], rbuf.at[src], as_.at[src], ar.at[src], head=h).wait_recv()
        return 0

    lax.fori_loop(1, 32, collect, 0)

    for q in range(32):
        asm[0:16, q * W:(q + 1) * W] = rbuf[q, :, 0:W]
        asm[16:32, q * W:(q + 1) * W] = rbuf[q, :, W:BB]
    for g in range(5):
        v = asm[:, g * 2048:(g + 1) * 2048].astype(F32)
        scale = lax.rsqrt(jnp.mean(v * v, axis=1, keepdims=True) + 1e-5)
        for k in range(16):
            c0 = g * 16 + k
            out[:, c0 * 128:(c0 + 1) * 128] = (
                v[:, k * 128:(k + 1) * 128] * scale * gain[c0:c0 + 1, :]).astype(BF16)

    for k in range(3):
        taps_copy(k).wait_send()
    for j in range(4):
        p = order[j]
        for sign in (1, -1):
            along(p, sign, lambda d: d.wait_send())
            for yy in (left, right, far):
                along_early(p, yy, sign, lambda d: d.wait_send())
        for kind in range(4):
            ring(p, kind, j == 0).wait_send()
        twin(p, y, True).wait_send()
        for yy in (left, right, far):
            twin(p, yy, j == 0).wait_send()
            if j:
                twin_early(p, yy).wait_send()
        for kind in range(3):
            share_copy(p, kind).wait_send()

    @pl.when(s < NSEQ - 1)
    def _():
        for copy in halo_copies():
            copy.wait_send()

    for t in range(1, NSEQ):
        @pl.when(s + t < NSEQ)
        def _():
            rcopy(sfin, st_in.at[s], ss.at[t], sr.at[s], seq=s).wait_send()
            rcopy(tfin, tot_in.at[s], ts.at[t], tr.at[s], seq=s).wait_send()

    def sent(k, _):
        dst = (h + k) % 32
        rcopy(sb.at[dst], rbuf.at[h], as_.at[dst], ar.at[h], head=h).wait_send()
        return 0

    lax.fori_loop(1, 32, sent, 0)


def call(tok, wx, wz, wbc, wdt, cx, cbc, bias, alog, skip, gain):
    d = tok.shape[1]
    anywhere = pl.BlockSpec(memory_space=pl.ANY)
    vm = pl.BlockSpec(memory_space=pltpu.VMEM)
    sm = pl.BlockSpec(memory_space=pltpu.SMEM)
    dma = pltpu.SemaphoreType.DMA
    mem = pltpu.VMEM
    return pl.pallas_call(
        kernel,
        out_shape=jax.ShapeDtypeStruct((32, 10240), BF16),
        in_specs=[anywhere] * 4 + [vm] * 3 + [sm] * 3 + [vm],
        out_specs=vm,
        scratch_shapes=[
            mem((32, 32, d), BF16), mem((BB + 80, d), BF16), mem((BB + 80, 256), F32),
            mem((BB, 1024), BF16), mem((16, 1024), F32), mem((256, 1024), BF16), mem((256, 1024), BF16),
            mem((16, 384), BF16), mem((16, 128), BF16), mem((16, 384), BF16), mem((4, 16, 128), BF16),
            mem((W + 256, 128), F32), mem((4, 8, 128), F32), mem((W, 1024), BF16),
            mem((64, 128), F32), mem((64, 128), F32), mem((128, 64), F32), mem((W, 1024), F32),
            mem((8, W, 128), F32), mem((W, 128), BF16), mem((8, 128), F32),
            mem((8, W, 128), BF16), mem((8, 8, 128), F32), mem((W, 128), F32),
            mem((32, 16, BB), BF16), mem((32, 16, BB), BF16), mem((32, 10240), BF16),
            dma((4,)), dma((4, 2)), dma((4,)), dma((4, 4, 2)), dma((4, 4)),
            dma((4, 4)), dma((4, 4)), dma((4, 4)), dma((4, 4)), dma((4, 4)), dma((4, 4)),
            dma((4, 3)), dma((4, 3)), dma((3,)), dma((4,)), dma, dma, dma((4,)), dma((4,)),
            dma((8,)), dma((8,)), dma((8,)), dma((8,)), dma((32,)), dma((32,)),
        ],
        compiler_params=pltpu.CompilerParams(collective_id=0, has_side_effects=True,
                                             vmem_limit_bytes=60 * 2**20),
        name="mixer",
    )(tok, wx, wz, wbc, wdt, cx, cbc, bias, alog, skip, gain.reshape(80, 128))


def shards(tokens, wx, wz, wbc, wdt, cx, cbc, bias, alog, skip, gain):
    return call(tokens, wx.T, wz.T, wbc.T, wdt.T, cx, cbc, bias, alog, skip, gain)


def solution(mesh):
    cols = P(None, "head")
    placed = (P(("seq", "head"), None), cols, cols, cols, cols, cols, cols,
              P("head"), P("head"), P("head"), P())
    return jax.shard_map(
        shards, mesh=mesh, in_specs=placed, out_specs=P(("seq", "head"), None), check_vma=False
    )
```

```python
import jax
import jax.numpy as jnp
from jax import lax
from jax.experimental import pallas as pl
from jax.experimental.pallas import tpu as pltpu
from jax.sharding import PartitionSpec as P

MESH = pl.DeviceIdType.MESH
F32 = jnp.float32
BF16 = jnp.bfloat16
NT = (((1,), (1,)), ((), ()))
TN = (((0,), (0,)), ((), ()))
KC = 4096
EARLY = 3328
HEADS = 5
W = 320
BB = 2 * W
FIRST = W + 80
NSEQ = 8


def rcopy(src, dst, send, recv, **device):
    return pltpu.make_async_remote_copy(
        src_ref=src, dst_ref=dst, send_sem=send, recv_sem=recv,
        device_id=device, device_id_type=MESH,
    )


def silu(v):
    return v / (1.0 + jnp.exp(-v))


def kernel(tok, wx, wz, wbc, wdt, cx, cbc, bias, alog, skip, gain, out,
           buf, wt, res, pre, dt, bcp, bcf, halo_x, halo_b, in_x, in_b, hpad, taps, xc,
           step, cums, cumt, yin, sstart, offs, sfin, tfin, st_mate, tot_mate, tail_s, tail_t, xfin, xtot, st_in, tot_in, inc, sb, rbuf, asm,
           lsem, zs, zr, es, er, ys, yr, ds, dr, fs, fr,
           bs, br, cs, cr, hxs, hxr, hbs, hbr, ss, sr, ts, tr, xs, xr, vs, vr, as_, ar):
    h = lax.axis_index("head")
    s = lax.axis_index("seq")
    z, y, c = h // 8, (h // 2) % 4, h % 2
    right, left, far = (y + 1) % 4, (y + 3) % 4, (y + 2) % 4
    sib = h + 1 - 2 * c
    across = h + 2 - 4 * (y % 2)
    base = (h // 4) * 4
    quarter = h % 4
    x, zh = s // 2, s % 2
    place = zh * 4 + z
    mate = s + 1 - 2 * zh
    ends = jnp.logical_or(place < 2, place >= 6)
    middle = jnp.logical_not(ends)
    first_run = jnp.where(ends, (place + 3) % 8, 4)
    turn = jnp.where(ends, 0, (place + 7) % 4)
    order = [z, (z + 1) % 4, (z + 3) % 4, (z + 2) % 4]

    def plane_in(slot):
        return (place + 7 + (slot - z + 5) % 4) % 8

    def owner(slot):
        return x * 2 + plane_in(slot) // 4

    def slot_of(k):
        return (turn + k) % 4

    def upward(dz):
        there = (place + dz + 8) % 8
        return dict(seq=x * 2 + there // 4, head=(there % 4) * 8 + y * 2 + c)

    def at(p, yy):
        return p * 8 + yy * 2 + c

    own = pltpu.make_async_copy(tok, buf.at[h], lsem.at[0])
    own.start()
    loads = [
        pltpu.make_async_copy(wx, wt.at[pl.ds(0, W)], lsem.at[1]),
        pltpu.make_async_copy(wz, wt.at[pl.ds(FIRST, W)], lsem.at[2]),
        pltpu.make_async_copy(wbc, wt.at[pl.ds(W, 64)], lsem.at[3]),
    ]
    barrier = pltpu.get_barrier_semaphore()

    def signal(**device):
        pl.semaphore_signal(barrier, inc=1, device_id=device, device_id_type=MESH)

    def greet(k, _):
        there = (place + 6 + k // 8) % 8
        who = (there % 4) * 8 + k % 8

        @pl.when(k != 16 + h % 8)
        def _():
            signal(seq=x * 2 + there // 4, head=who)

        return 0

    lax.fori_loop(0, 32, greet, 0)
    for k in range(1, 4):
        signal(seq=(s + 2 * k) % NSEQ)
    for k in range(4):
        signal(seq=mate, head=base + k)
    joined = jnp.logical_and(z == 1, middle)
    alone = jnp.logical_and(z == 1, ends)
    hand_on = jnp.logical_and(x < 3, jnp.logical_not(alone))
    next_seq = jnp.where(joined, mate + 2, s + 2)
    prev_seq = jnp.where(alone, mate - 2, s - 2)

    @pl.when(jnp.logical_and(x > 0, ends))
    def _():
        for k in range(4):
            signal(seq=prev_seq, head=base + k)

    hands_on = jnp.logical_and(hand_on, jnp.logical_or(ends, joined))
    pl.semaphore_wait(barrier, 31 + 3 + 4 + 4 * hands_on.astype(jnp.int32))
    own.wait()

    early = pl.ds(0, EARLY)
    late = pl.ds(EARLY, buf.shape[2] - EARLY)

    def along(p, sign):
        slot = buf.at[at(p, y)]
        return rcopy(slot, slot, zs.at[p, (sign + 1) // 2], zr.at[p], **upward(sign))

    def along_early(p, yy, sign):
        slot = buf.at[at(p, yy), :, early]
        return rcopy(slot, slot, es.at[p, yy, (sign + 1) // 2], er.at[p, yy], **upward(sign))

    def ring(p, kind, own_plane):
        cols = pl.ds(0, buf.shape[2]) if own_plane else late
        yy, rows, to = (
            (y, pl.ds(0, 32), right), (y, pl.ds(0, 32), left),
            (left, pl.ds(0, 16), right), (right, pl.ds(16, 16), left),
        )[kind]
        part = buf.at[at(p, yy), rows, cols]
        return rcopy(part, part, ys.at[p, kind], yr.at[p, kind], head=at(z, to))

    def ring_wait(p, kind, own_plane):
        cols = pl.ds(0, buf.shape[2]) if own_plane else late
        yy, rows = ((left, pl.ds(0, 32)), (right, pl.ds(0, 32)),
                    (far, pl.ds(0, 16)), (far, pl.ds(16, 16)))[kind]
        part = buf.at[at(p, yy), rows, cols]
        rcopy(part, part, ys.at[p, kind], yr.at[p, kind], head=h).wait_recv()

    def twin(p, yy, whole):
        slot = buf.at[at(p, yy)] if whole else buf.at[at(p, yy), :, late]
        return rcopy(slot, slot, ds.at[p, yy], dr.at[p, yy], head=sib)

    def twin_wait(p, yy, whole):
        slot = buf.at[p * 8 + yy * 2 + 1 - c]
        slot = slot if whole else slot.at[:, late]
        rcopy(slot, slot, ds.at[p, yy], dr.at[p, yy], head=h).wait_recv()

    def twin_early(p, yy):
        slot = buf.at[at(p, yy), :, early]
        return rcopy(slot, slot, fs.at[p, yy], fr.at[p, yy], head=sib)

    def twin_early_wait(p, yy):
        slot = buf.at[p * 8 + yy * 2 + 1 - c, :, early]
        rcopy(slot, slot, fs.at[p, yy], fr.at[p, yy], head=h).wait_recv()

    def begin(p, own_plane):
        ring(p, 0, own_plane).start()
        ring(p, 1, own_plane).start()
        twin(p, y, True).start()

    def arrive(j):
        p = order[j]
        slot = buf.at[at(p, y)]
        rcopy(slot, slot, zs.at[p, 0], zr.at[p], head=h).wait_recv()
        if j == 1:
            along(p, -1).start()
        begin(p, False)

    def arrive_early(j):
        p = order[j]
        for yy in (left, right, far):
            slot = buf.at[at(p, yy), :, early]
            rcopy(slot, slot, es.at[p, yy, 0], er.at[p, yy], head=h).wait_recv()
            if j == 1:
                along_early(p, yy, -1).start()
            twin_early(p, yy).start()

    def near(p, own_plane):
        ring_wait(p, 0, own_plane)
        ring(p, 2, own_plane).start()
        ring_wait(p, 1, own_plane)
        ring(p, 3, own_plane).start()
        for yy in (left, right):
            twin(p, yy, own_plane).start()
            if own_plane:
                along_early(p, yy, -1).start()
                along_early(p, yy, 1).start()

    def last(p, own_plane):
        ring_wait(p, 2, own_plane)
        ring_wait(p, 3, own_plane)
        twin(p, far, own_plane).start()
        if own_plane:
            along_early(p, far, -1).start()
            along_early(p, far, 1).start()

    def complete(p, own_plane):
        twin_wait(p, y, True)
        for yy in (left, right, far):
            twin_wait(p, yy, own_plane)
            if not own_plane:
                twin_early_wait(p, yy)

    def product(p, r0, n):
        def chunk(k, _):
            ks = pl.ds(pl.multiple_of(k * KC, KC), KC)
            a = buf[pl.ds(p * 8, 8), :, ks].reshape(256, KC)
            part = lax.dot_general(wt[r0:r0 + n, ks], a, NT, preferred_element_type=F32)

            @pl.when(k == 0)
            def _():
                res[r0:r0 + n] = part

            @pl.when(k > 0)
            def _():
                res[r0:r0 + n] += part

            return 0

        lax.fori_loop(0, buf.shape[2] // KC, chunk, 0)

    def span_of(p):
        return pl.ds(pl.multiple_of(p * 256, 256), 256)

    def quarter_rows(q):
        return pl.ds(pl.multiple_of(q * 64, 64), 64)

    q_sib = quarter + 1 - 2 * c
    q_across = quarter + 2 - 4 * (y % 2)
    q_other = q_across + 1 - 2 * c

    def share_copy(p, kind):
        q = (quarter, quarter, q_across)[kind]
        part = bcp.at[quarter_rows(q), span_of(p)]
        return rcopy(part, part, bs.at[p, kind], br.at[p, kind], head=(sib, across, sib)[kind])

    def share_wait(p, kind):
        q = (q_sib, q_across, q_other)[kind]
        part = bcp.at[quarter_rows(q), span_of(p)]
        rcopy(part, part, bs.at[p, kind], br.at[p, kind], head=h).wait_recv()

    def store_bc(p):
        span = span_of(p)
        bcp[quarter_rows(quarter), span] = res[W:W + 64].astype(BF16)
        dt[:, span] = res[W + 64:FIRST]
        share_copy(p, 0).start()
        share_copy(p, 1).start()

    def pass_bc(p):
        share_wait(p, 1)
        share_copy(p, 2).start()

    def store_x(p):
        pre[0:W, span_of(p)] = res[0:W].astype(BF16)

    def store_z(p):
        pre[W:BB, span_of(p)] = res[FIRST:FIRST + W].astype(BF16)

    pick = (lax.broadcasted_iota(jnp.int32, (16, 128), 1)
            == lax.broadcasted_iota(jnp.int32, (16, 128), 0) + 112).astype(BF16)

    def halo_copies(i):
        if i == 0:
            to, slot = jnp.where(joined, next_seq, mate), jnp.where(jnp.logical_or(ends, joined), 0, 1)
        else:
            to, slot = next_seq, 0
        yield rcopy(halo_x.at[i], in_x.at[slot], hxs.at[i], hxr.at[slot], seq=to)
        for k in range(4):
            yield rcopy(halo_b.at[i], in_b.at[slot, quarter], hbs.at[i, k], hbr.at[slot, quarter],
                        seq=to, head=base + k)

    halo_when = (jnp.logical_or(jnp.logical_not(joined), x < 3), jnp.logical_and(ends, hand_on))
    halo_slot = (order[3], 3)

    def send_halo(p):
        for i in range(2):
            @pl.when(jnp.logical_and(p == halo_slot[i], halo_when[i]))
            def _():
                tail = pl.ds(pl.multiple_of(p * 256 + 128, 128), 128)
                halo_x[i, :, 0:W] = lax.dot_general(
                    pick, pre[0:W, tail], NT, preferred_element_type=F32).astype(BF16)
                halo_b[i, :, 0:64] = lax.dot_general(
                    pick, bcp[quarter_rows(quarter), tail], NT, preferred_element_type=F32).astype(BF16)
                for copy in halo_copies(i):
                    copy.start()

    def project(p, own_plane):
        complete(p, own_plane)
        product(p, 0, FIRST)
        store_bc(p)
        store_x(p)
        send_halo(p)

    def gates(p):
        product(p, FIRST, W)
        store_z(p)

    def taps_copy(k):
        slot = taps.at[quarter]
        return rcopy(slot, slot, cs.at[k], cr.at[quarter], head=base + (h + k + 1) % 4)

    def taps_wait(k):
        q = (h + k + 1) % 4
        rcopy(taps.at[q], taps.at[q], cs.at[k], cr.at[q], head=h).wait_recv()

    along(order[0], -1).start()
    along(order[0], 1).start()
    begin(order[0], True)
    for load in loads:
        load.start()
    taps[quarter, 0:4, 0:64] = cbc[...]
    for k in range(3):
        taps_copy(k).start()
    wt[W + 64:FIRST, :] = jnp.concatenate(
        [wdt[...].astype(F32), jnp.zeros((16 - HEADS, wt.shape[1]), F32)], axis=0).astype(BF16)
    halo_x[...] = jnp.zeros_like(halo_x)
    halo_b[...] = jnp.zeros_like(halo_b)
    for load in loads:
        load.wait()

    arrive(1)
    near(order[0], True)
    arrive(2)
    last(order[0], True)
    near(order[1], False)
    project(order[0], True)
    arrive_early(2)
    near(order[2], False)
    last(order[1], False)
    arrive_early(1)
    arrive(3)
    gates(order[0])
    last(order[2], False)
    project(order[1], False)
    gates(order[1])
    near(order[3], False)
    project(order[2], False)
    pass_bc(order[0])
    arrive_early(3)
    last(order[3], False)
    pass_bc(order[1])
    pass_bc(order[2])
    project(order[3], False)

    def cols_of(b):
        return pl.ds(pl.multiple_of(slot_of(b // 2) * 256 + (b % 2) * 128, 128), 128)

    row = lax.broadcasted_iota(jnp.int32, (8, 128), 0)
    bias_col = jnp.zeros((8, 128), F32)
    rate_col = jnp.zeros((8, 128), F32)
    for k in range(HEADS):
        bias_col = jnp.where(row == k, bias[k], bias_col)
        rate_col = jnp.where(row == k, alog[k], rate_col)
    rate_col = jnp.exp(rate_col)
    upper = (lax.broadcasted_iota(jnp.int32, (128, 128), 0)
             <= lax.broadcasted_iota(jnp.int32, (128, 128), 1))
    parts = []
    for b in range(8):
        v = dt[0:8, cols_of(b)] + bias_col
        v = jnp.maximum(v, 0.0) + jnp.log1p(jnp.exp(-jnp.abs(v)))
        step[b * 8:(b + 1) * 8, :] = v
        parts.append(-v * rate_col)
    dec = jnp.concatenate(parts, axis=0)
    cum = jnp.dot(dec, upper.astype(F32), preferred_element_type=F32, precision=lax.Precision.HIGHEST)
    cums[...] = cum
    tot = jnp.broadcast_to(cum[:, 127:128], (64, 128))
    weight = step[...] * jnp.exp(tot - cum)
    cumt[...] = (cum - jnp.log(step[...])).T

    lane = lax.broadcasted_iota(jnp.int32, (64, 128), 1)
    tapx = jnp.concatenate([cx[...], jnp.zeros((4, W), F32)], axis=0).T

    def conv_block(src, r0, taps, prev, b, dst, to):
        cur = src[r0:r0 + 64, cols_of(b)].astype(F32)
        total = taps[:, 3:4] * cur
        for k in range(1, 4):
            moved = pltpu.roll(jnp.where(lane >= 128 - k, prev, cur), k, 1)
            total = total + taps[:, 3 - k:4 - k] * moved
        dst[r0:r0 + 64, to] = silu(total).astype(BF16)
        return cur

    def conv(src, r0, taps, dst):
        prev = src[r0:r0 + 64, cols_of(0)].astype(F32)
        for b in range(1, 8):
            prev = conv_block(src, r0, taps, prev, b, dst, slice(b * 128, (b + 1) * 128))

    for k in range(HEADS):
        conv(pre, k * 64, tapx[k * 64:(k + 1) * 64], xc)
    gates(order[2])
    pass_bc(order[3])
    for k in range(3):
        taps_wait(k)
    tapb = [taps[q].T[0:64] for q in range(4)]
    for p in range(4):
        share_wait(p, 0)
        share_wait(p, 2)
    for q in range(4):
        conv(bcp, q * 64, tapb[q], bcf)

    def starts(i, b):
        to = pl.ds(pl.multiple_of(b * 128, 128), 128)
        for k in range(HEADS):
            conv_block(pre, k * 64, tapx[k * 64:(k + 1) * 64], hpad[i, k * 64:(k + 1) * 64, :], b, xc, to)
        for q in range(4):
            conv_block(bcp, q * 64, tapb[q], hpad[i, W + q * 64:W + (q + 1) * 64, :], b, bcf, to)

    halo_due = (jnp.logical_or(middle, x > 0), jnp.logical_and(ends, z != 1))
    hpad[0] = jnp.zeros((W + 256, 128), F32)
    for i in range(2):
        @pl.when(halo_due[i])
        def _():
            rcopy(halo_x.at[i], in_x.at[i], hxs.at[i], hxr.at[i], seq=s).wait_recv()
            hpad[i, 0:W, :] = lax.dot_general(in_x[i, :, 0:W], pick, TN, preferred_element_type=F32)
            for q in range(4):
                rcopy(halo_b.at[i], in_b.at[i, q], hbs.at[i, 0], hbr.at[i, q], seq=s).wait_recv()
                hpad[i, W + q * 64:W + q * 64 + 64, :] = lax.dot_general(
                    in_b[i, q, :, 0:64], pick, TN, preferred_element_type=F32)
            if i:
                starts(1, 2 * first_run)

    starts(0, 0)

    def rows(v, r):
        return jnp.concatenate(
            [jnp.broadcast_to(v[r + k:r + k + 1, :], (64, 128)) for k in range(HEADS)], axis=0)

    def mate_copy(i):
        return rcopy(sfin.at[i], st_mate.at[i], ss.at[i], sr.at[i], seq=mate)

    def mate_total(i):
        return rcopy(tfin.at[i], tot_mate.at[i], ts.at[i], tr.at[i], seq=mate)

    state = jnp.zeros((W, 128), F32)
    total = jnp.zeros((8, 128), F32)
    for k in range(4):
        if k:
            @pl.when(first_run == k)
            def _():
                sfin[0] = state.astype(BF16)
                tfin[0] = total
                mate_copy(0).start()
                mate_total(0).start()

            state = jnp.where(first_run == k, 0.0, state)
            total = jnp.where(first_run == k, 0.0, total)
        for b in (2 * k, 2 * k + 1):
            cols = slice(b * 128, (b + 1) * 128)
            sstart[b] = state
            offs[b] = total
            xw = (xc[:, cols].astype(F32) * rows(weight, b * 8)).astype(BF16)
            fresh = lax.dot_general(xw, bcf[0:128, cols], NT, preferred_element_type=F32)
            tb = tot[b * 8:(b + 1) * 8, :]
            state = state * rows(jnp.exp(tb), 0) + fresh
            total = total + tb

    @pl.when(first_run == 4)
    def _():
        sfin[0] = state.astype(BF16)
        tfin[0] = total
        mate_copy(0).start()
        mate_total(0).start()
        sfin[1] = jnp.zeros((W, 128), BF16)
        tfin[1] = jnp.zeros((8, 128), F32)

    @pl.when(first_run < 4)
    def _():
        sfin[1] = state.astype(BF16)
        tfin[1] = total

    @pl.when(ends)
    def _():
        mate_copy(1).start()
        mate_total(1).start()

    gates(order[3])
    for b in range(8):
        cols = slice(b * 128, (b + 1) * 128)
        scores = lax.dot_general(bcf[0:128, cols], bcf[128:256, cols], TN, preferred_element_type=F32)
        scores = jnp.where(upper, scores, 0.0)
        for k in range(HEADS):
            r = b * 8 + k
            diff = cums[r:r + 1, :] - cumt[:, r:r + 1]
            mixing = jnp.exp(jnp.where(upper, diff, -jnp.inf)) * scores
            yin[k * 64:(k + 1) * 64, cols] = jnp.dot(
                xc[k * 64:(k + 1) * 64, cols], mixing.astype(BF16), preferred_element_type=F32)

    mate_copy(0).wait_recv()
    mate_total(0).wait_recv()

    @pl.when(middle)
    def _():
        mate_copy(1).wait_recv()
        mate_total(1).wait_recv()

    def grown(v, t):
        return v * rows(jnp.exp(t), 0)

    head_s = jnp.where(ends, sfin[0].astype(F32), st_mate[0].astype(F32))
    head_t = jnp.where(ends, tfin[0], tot_mate[0])
    mid_s = jnp.where(ends, st_mate[0].astype(F32), sfin[0].astype(F32))
    mid_t = jnp.where(ends, tot_mate[0], tfin[0])

    @pl.when(middle)
    def _():
        tail_s[...] = st_mate[1].astype(F32)
        tail_t[...] = tot_mate[1]

    @pl.when(ends)
    def _():
        tail_s[...] = sfin[1].astype(F32)
        tail_t[...] = tfin[1]

    xfin[...] = (grown(grown(head_s, mid_t) + mid_s, tail_t[...]) + tail_s[...]).astype(BF16)
    xtot[...] = head_t + mid_t + tail_t[...]
    for t in range(1, 4):
        @pl.when(x + t < 4)
        def _():
            rcopy(xfin, st_in.at[x], xs.at[t], xr.at[x], seq=s + 2 * t).start()
            rcopy(xtot, tot_in.at[x], vs.at[t], vr.at[x], seq=s + 2 * t).start()

    inc[0] = jnp.zeros((W, 128), F32)
    for q in range(3):
        @pl.when(q < x)
        def _():
            rcopy(xfin, st_in.at[q], xs.at[0], xr.at[q], seq=s).wait_recv()
            rcopy(xtot, tot_in.at[q], vs.at[0], vr.at[q], seq=s).wait_recv()
            inc[0] = grown(inc[0], tot_in[q]) + st_in[q].astype(F32)

    after_head = grown(inc[0], head_t) + head_s
    inc[1] = grown(after_head, mid_t) + mid_s

    @pl.when(middle)
    def _():
        inc[0] = after_head

    skips = jnp.concatenate([jnp.full((64, 128), skip[k], F32) for k in range(HEADS)], axis=0)
    for b in range(8):
        cols = slice(b * 128, (b + 1) * 128)
        run = jnp.where(first_run <= b // 2, 1, 0)
        st = (sstart[b] + inc[run] * rows(jnp.exp(offs[b]), 0)).astype(BF16)
        yst = jnp.dot(st, bcf[128:256, cols], preferred_element_type=F32)
        yv = yin[:, cols] + yst * rows(jnp.exp(cums[b * 8:(b + 1) * 8, :]), 0) + skips * xc[:, cols].astype(F32)
        yv = yv.astype(BF16).astype(F32)
        g = (yv * silu(pre[W:BB, cols_of(b)].astype(F32))).T
        for i in range(4):
            dst = slot_of(b // 2) * 8 + 4 * (b % 2) + i
            sb[dst, :, 0:W] = g[32 * i:32 * i + 16, :].astype(BF16)
            sb[dst, :, W:BB] = g[32 * i + 16:32 * i + 32, :].astype(BF16)

    def scatter(k, _):
        dst = (h + 16 + k) % 32

        @pl.when(k != 16)
        def _():
            rcopy(sb.at[dst], rbuf.at[h], as_.at[dst], ar.at[h], seq=owner(dst // 8), head=dst).start()

        return 0

    lax.fori_loop(0, 32, scatter, 0)
    rbuf[h] = sb[h]

    def collect(k, _):
        src = (h + k) % 32
        rcopy(sb.at[src], rbuf.at[src], as_.at[src], ar.at[src], head=h).wait_recv()
        return 0

    lax.fori_loop(1, 32, collect, 0)

    for q in range(32):
        asm[0:16, q * W:(q + 1) * W] = rbuf[q, :, 0:W]
        asm[16:32, q * W:(q + 1) * W] = rbuf[q, :, W:BB]
    for g in range(5):
        v = asm[:, g * 2048:(g + 1) * 2048].astype(F32)
        scale = lax.rsqrt(jnp.mean(v * v, axis=1, keepdims=True) + 1e-5)
        for k in range(16):
            c0 = g * 16 + k
            out[:, c0 * 128:(c0 + 1) * 128] = (
                v[:, k * 128:(k + 1) * 128] * scale * gain[c0:c0 + 1, :]).astype(BF16)

    for k in range(3):
        taps_copy(k).wait_send()
    for j in range(4):
        p = order[j]
        for sign in (-1, 1)[:2 if j == 0 else 1 if j == 1 else 0]:
            along(p, sign).wait_send()
            for yy in (left, right, far):
                along_early(p, yy, sign).wait_send()
        for kind in range(4):
            ring(p, kind, j == 0).wait_send()
        twin(p, y, True).wait_send()
        for yy in (left, right, far):
            twin(p, yy, j == 0).wait_send()
            if j:
                twin_early(p, yy).wait_send()
        for kind in range(3):
            share_copy(p, kind).wait_send()

    for i in range(2):
        @pl.when(halo_when[i])
        def _():
            for copy in halo_copies(i):
                copy.wait_send()

    mate_copy(0).wait_send()
    mate_total(0).wait_send()

    @pl.when(ends)
    def _():
        mate_copy(1).wait_send()
        mate_total(1).wait_send()

    for t in range(1, 4):
        @pl.when(x + t < 4)
        def _():
            rcopy(xfin, st_in.at[x], xs.at[t], xr.at[x], seq=s).wait_send()
            rcopy(xtot, tot_in.at[x], vs.at[t], vr.at[x], seq=s).wait_send()

    def sent(k, _):
        dst = (h + k) % 32
        rcopy(sb.at[dst], rbuf.at[h], as_.at[dst], ar.at[h], head=h).wait_send()
        return 0

    lax.fori_loop(1, 32, sent, 0)


def call(tok, wx, wz, wbc, wdt, cx, cbc, bias, alog, skip, gain):
    d = tok.shape[1]
    anywhere = pl.BlockSpec(memory_space=pl.ANY)
    vm = pl.BlockSpec(memory_space=pltpu.VMEM)
    sm = pl.BlockSpec(memory_space=pltpu.SMEM)
    dma = pltpu.SemaphoreType.DMA
    mem = pltpu.VMEM
    return pl.pallas_call(
        kernel,
        out_shape=jax.ShapeDtypeStruct((32, 10240), BF16),
        in_specs=[anywhere] * 4 + [vm] * 3 + [sm] * 3 + [vm],
        out_specs=vm,
        scratch_shapes=[
            mem((32, 32, d), BF16), mem((BB + 80, d), BF16), mem((BB + 80, 256), F32),
            mem((BB, 1024), BF16), mem((16, 1024), F32), mem((256, 1024), BF16), mem((256, 1024), BF16),
            mem((2, 16, 384), BF16), mem((2, 16, 128), BF16), mem((2, 16, 384), BF16), mem((2, 4, 16, 128), BF16),
            mem((2, W + 256, 128), F32), mem((4, 8, 128), F32), mem((W, 1024), BF16),
            mem((64, 128), F32), mem((64, 128), F32), mem((128, 64), F32), mem((W, 1024), F32),
            mem((8, W, 128), F32), mem((8, 8, 128), F32), mem((2, W, 128), BF16), mem((2, 8, 128), F32),
            mem((2, W, 128), BF16), mem((2, 8, 128), F32), mem((W, 128), F32), mem((8, 128), F32),
            mem((W, 128), BF16), mem((8, 128), F32),
            mem((3, W, 128), BF16), mem((3, 8, 128), F32), mem((2, W, 128), F32),
            mem((32, 16, BB), BF16), mem((32, 16, BB), BF16), mem((32, 10240), BF16),
            dma((4,)), dma((4, 2)), dma((4,)), dma((4, 4, 2)), dma((4, 4)),
            dma((4, 4)), dma((4, 4)), dma((4, 4)), dma((4, 4)), dma((4, 4)), dma((4, 4)),
            dma((4, 3)), dma((4, 3)), dma((3,)), dma((4,)), dma((2,)), dma((2,)), dma((2, 4)), dma((2, 4)),
            dma((2,)), dma((2,)), dma((2,)), dma((2,)), dma((4,)), dma((3,)), dma((4,)), dma((3,)),
            dma((32,)), dma((32,)),
        ],
        compiler_params=pltpu.CompilerParams(collective_id=0, has_side_effects=True,
                                             vmem_limit_bytes=60 * 2**20),
        name="mixer",
    )(tok, wx, wz, wbc, wdt, cx, cbc, bias, alog, skip, gain.reshape(80, 128))


def shards(tokens, wx, wz, wbc, wdt, cx, cbc, bias, alog, skip, gain):
    return call(tokens, wx.T, wz.T, wbc.T, wdt.T, cx, cbc, bias, alog, skip, gain)


def solution(mesh):
    cols = P(None, "head")
    placed = (P(("seq", "head"), None), cols, cols, cols, cols, cols, cols,
              P("head"), P("head"), P("head"), P())
    return jax.shard_map(
        shards, mesh=mesh, in_specs=placed, out_specs=P(("seq", "head"), None), check_vma=False
    )
```

```python
import jax
import jax.numpy as jnp
from jax import lax
from jax.experimental import pallas as pl
from jax.experimental.pallas import tpu as pltpu
from jax.sharding import PartitionSpec as P

MESH = pl.DeviceIdType.MESH
F32 = jnp.float32
BF16 = jnp.bfloat16
NT = (((1,), (1,)), ((), ()))
TN = (((0,), (0,)), ((), ()))
KC = 4096
EARLY = 3072
HEADS = 5
W = 320
BB = 2 * W
FIRST = W + 80
NSEQ = 8


def rcopy(src, dst, send, recv, **device):
    return pltpu.make_async_remote_copy(
        src_ref=src, dst_ref=dst, send_sem=send, recv_sem=recv,
        device_id=device, device_id_type=MESH,
    )


def silu(v):
    return v / (1.0 + jnp.exp(-v))


def kernel(tok, wx, wz, wbc, wdt, cx, cbc, bias, alog, skip, rbuf,
           wdt_v, cx_v, cbc_v, buf, wt, res, pre, dt, bcp, bcf, halo_x, halo_b, in_x, in_b, hpad, taps, xc,
           step, cums, cumt, yin, sstart, offs, sfin, tfin, st_mate, tot_mate, own_s, xfin, xtot, st_in, tot_in, inc, sb,
           lsem, zs, zr, es, er, ys, yr, ds, dr, fs, fr,
           bs, br, cs, cr, hxs, hxr, hbs, hbr, ss, sr, ts, tr, xs, xr, vs, vr, as_, ar):
    h = lax.axis_index("head")
    s = lax.axis_index("seq")
    z, y, c = h // 8, (h // 2) % 4, h % 2
    right, left, far = (y + 1) % 4, (y + 3) % 4, (y + 2) % 4
    sib = h + 1 - 2 * c
    across = h + 2 - 4 * (y % 2)
    base = (h // 4) * 4
    quarter = h % 4
    x, zh = s // 2, s % 2
    place = zh * 4 + z
    mate = s + 1 - 2 * zh
    ends = jnp.logical_or(place < 2, place >= 6)
    middle = jnp.logical_not(ends)
    first_run = jnp.where(ends, (place + 3) % 8, 4)
    turn = jnp.where(ends, 0, (place + 7) % 4)
    order = [z, (z + 1) % 4, (z + 3) % 4, (z + 2) % 4]

    def plane_in(slot):
        return (place + 7 + (slot - z + 5) % 4) % 8

    def owner(slot):
        return x * 2 + plane_in(slot) // 4

    def slot_of(k):
        return (turn + k) % 4

    def upward(dz):
        there = (place + dz + 8) % 8
        return dict(seq=x * 2 + there // 4, head=(there % 4) * 8 + y * 2 + c)

    def at(p, yy):
        return p * 8 + yy * 2 + c

    own = pltpu.make_async_copy(tok, buf.at[h], lsem.at[0])
    own.start()
    loads = [
        pltpu.make_async_copy(wx, wt.at[pl.ds(0, W)], lsem.at[1]),
        pltpu.make_async_copy(wz, wt.at[pl.ds(FIRST, W)], lsem.at[2]),
        pltpu.make_async_copy(wbc, wt.at[pl.ds(W, 64)], lsem.at[3]),
    ]
    smalls = [pltpu.make_async_copy(src, dst, lsem.at[4 + i])
              for i, (src, dst) in enumerate(((wdt, wdt_v), (cx, cx_v), (cbc, cbc_v)))]
    barrier = pltpu.get_barrier_semaphore()

    def signal(**device):
        pl.semaphore_signal(barrier, inc=1, device_id=device, device_id_type=MESH)

    def greet(k, _):
        there = (place + 6 + k // 8) % 8
        who = (there % 4) * 8 + k % 8

        @pl.when(k != 16 + h % 8)
        def _():
            signal(seq=x * 2 + there // 4, head=who)

        return 0

    lax.fori_loop(0, 32, greet, 0)
    for k in range(1, 4):
        signal(seq=(s + 2 * k) % NSEQ)
    for k in range(4):
        signal(seq=mate, head=base + k)
    joined = jnp.logical_and(z == 1, middle)
    alone = jnp.logical_and(z == 1, ends)
    hand_on = jnp.logical_and(x < 3, jnp.logical_not(alone))
    next_seq = jnp.where(joined, mate + 2, s + 2)
    prev_seq = jnp.where(alone, mate - 2, s - 2)

    @pl.when(jnp.logical_and(x > 0, ends))
    def _():
        for k in range(4):
            signal(seq=prev_seq, head=base + k)

    hands_on = jnp.logical_and(hand_on, jnp.logical_or(ends, joined))
    pl.semaphore_wait(barrier, 31 + 3 + 4 + 4 * hands_on.astype(jnp.int32))
    early = pl.ds(0, EARLY)
    late = pl.ds(EARLY, buf.shape[2] - EARLY)

    def along(p, sign, own_plane):
        slot = buf.at[at(p, y)]
        return rcopy(tok if own_plane else slot, slot, zs.at[p, (sign + 1) // 2], zr.at[p], **upward(sign))

    def along_early(p, yy, sign):
        slot = buf.at[at(p, yy), :, early]
        return rcopy(slot, slot, es.at[p, yy, (sign + 1) // 2], er.at[p, yy], **upward(sign))

    def ring(p, kind, own_plane):
        cols = pl.ds(0, buf.shape[2]) if own_plane else late
        yy, rows, to = (
            (y, pl.ds(0, 32), right), (y, pl.ds(0, 32), left),
            (left, pl.ds(0, 16), right), (right, pl.ds(16, 16), left),
        )[kind]
        part = buf.at[at(p, yy), rows, cols]
        src = tok if own_plane and kind < 2 else part
        return rcopy(src, part, ys.at[p, kind], yr.at[p, kind], head=at(z, to))

    def ring_wait(p, kind, own_plane):
        cols = pl.ds(0, buf.shape[2]) if own_plane else late
        yy, rows = ((left, pl.ds(0, 32)), (right, pl.ds(0, 32)),
                    (far, pl.ds(0, 16)), (far, pl.ds(16, 16)))[kind]
        part = buf.at[at(p, yy), rows, cols]
        rcopy(part, part, ys.at[p, kind], yr.at[p, kind], head=h).wait_recv()

    def twin(p, yy, whole, mine=False):
        slot = buf.at[at(p, yy)] if whole else buf.at[at(p, yy), :, late]
        return rcopy(tok if mine else slot, slot, ds.at[p, yy], dr.at[p, yy], head=sib)

    def twin_wait(p, yy, whole):
        slot = buf.at[p * 8 + yy * 2 + 1 - c]
        slot = slot if whole else slot.at[:, late]
        rcopy(slot, slot, ds.at[p, yy], dr.at[p, yy], head=h).wait_recv()

    def twin_early(p, yy):
        slot = buf.at[at(p, yy), :, early]
        return rcopy(slot, slot, fs.at[p, yy], fr.at[p, yy], head=sib)

    def twin_early_wait(p, yy):
        slot = buf.at[p * 8 + yy * 2 + 1 - c, :, early]
        rcopy(slot, slot, fs.at[p, yy], fr.at[p, yy], head=h).wait_recv()

    def begin(p, own_plane):
        ring(p, 0, own_plane).start()
        ring(p, 1, own_plane).start()
        twin(p, y, True, own_plane).start()

    def arrive(j):
        p = order[j]
        slot = buf.at[at(p, y)]
        rcopy(slot, slot, zs.at[p, 0], zr.at[p], head=h).wait_recv()
        if j == 1:
            along(p, -1, False).start()
        begin(p, False)

    def arrive_early(j):
        p = order[j]
        for yy in (left, right, far):
            slot = buf.at[at(p, yy), :, early]
            rcopy(slot, slot, es.at[p, yy, 0], er.at[p, yy], head=h).wait_recv()
            if j == 1:
                along_early(p, yy, -1).start()
            twin_early(p, yy).start()

    def near(p, own_plane):
        ring_wait(p, 0, own_plane)
        ring(p, 2, own_plane).start()
        ring_wait(p, 1, own_plane)
        ring(p, 3, own_plane).start()
        for yy in (left, right):
            twin(p, yy, own_plane).start()
            if own_plane:
                along_early(p, yy, -1).start()
                along_early(p, yy, 1).start()

    def last(p, own_plane):
        ring_wait(p, 2, own_plane)
        ring_wait(p, 3, own_plane)
        twin(p, far, own_plane).start()
        if own_plane:
            along_early(p, far, -1).start()
            along_early(p, far, 1).start()

    def complete_early(p):
        twin_wait(p, y, True)
        for yy in (left, right, far):
            twin_early_wait(p, yy)

    def complete_late(p):
        for yy in (left, right, far):
            twin_wait(p, yy, False)

    def complete(p, own_plane):
        if own_plane:
            for yy in (y, left, right, far):
                twin_wait(p, yy, True)
        else:
            complete_early(p)
            complete_late(p)

    def product(p, r0, n, parts=((0, KC), (KC, KC))):
        for k0, count in parts:
            a = buf[pl.ds(p * 8, 8), :, k0:k0 + count].reshape(256, count)
            part = lax.dot_general(wt[r0:r0 + n, k0:k0 + count], a, NT, preferred_element_type=F32)
            res[r0:r0 + n] = part if k0 == 0 else res[r0:r0 + n] + part

    def span_of(p):
        return pl.ds(pl.multiple_of(p * 256, 256), 256)

    def quarter_rows(q):
        return pl.ds(pl.multiple_of(q * 64, 64), 64)

    q_sib = quarter + 1 - 2 * c
    q_across = quarter + 2 - 4 * (y % 2)
    q_other = q_across + 1 - 2 * c

    def share_copy(p, kind):
        q = (quarter, quarter, q_across)[kind]
        part = bcp.at[quarter_rows(q), span_of(p)]
        return rcopy(part, part, bs.at[p, kind], br.at[p, kind], head=(sib, across, sib)[kind])

    def share_wait(p, kind):
        q = (q_sib, q_across, q_other)[kind]
        part = bcp.at[quarter_rows(q), span_of(p)]
        rcopy(part, part, bs.at[p, kind], br.at[p, kind], head=h).wait_recv()

    def store_bc(p):
        span = span_of(p)
        bcp[quarter_rows(quarter), span] = res[W:W + 64].astype(BF16)
        dt[:, span] = res[W + 64:FIRST]
        share_copy(p, 0).start()
        share_copy(p, 1).start()

    def pass_bc(p):
        share_wait(p, 1)
        share_copy(p, 2).start()

    def store_x(p):
        pre[0:W, span_of(p)] = res[0:W].astype(BF16)

    def store_z(p):
        pre[W:BB, span_of(p)] = res[FIRST:FIRST + W].astype(BF16)

    pick = (lax.broadcasted_iota(jnp.int32, (16, 128), 1)
            == lax.broadcasted_iota(jnp.int32, (16, 128), 0) + 112).astype(BF16)

    def halo_copies(i):
        if i == 0:
            to, slot = jnp.where(joined, next_seq, mate), jnp.where(jnp.logical_or(ends, joined), 0, 1)
        else:
            to, slot = next_seq, 0
        yield rcopy(halo_x.at[i], in_x.at[slot], hxs.at[i], hxr.at[slot], seq=to)
        for k in range(4):
            yield rcopy(halo_b.at[i], in_b.at[slot, quarter], hbs.at[i, k], hbr.at[slot, quarter],
                        seq=to, head=base + k)

    halo_when = (jnp.logical_or(jnp.logical_not(joined), x < 3), jnp.logical_and(ends, hand_on))
    halo_slot = (order[3], 3)

    def send_halo(p):
        for i in range(2):
            @pl.when(jnp.logical_and(p == halo_slot[i], halo_when[i]))
            def _():
                tail = pl.ds(pl.multiple_of(p * 256 + 128, 128), 128)
                halo_x[i, :, 0:W] = lax.dot_general(
                    pick, pre[0:W, tail], NT, preferred_element_type=F32).astype(BF16)
                halo_b[i, :, 0:64] = lax.dot_general(
                    pick, bcp[quarter_rows(quarter), tail], NT, preferred_element_type=F32).astype(BF16)
                for copy in halo_copies(i):
                    copy.start()

    def store_first(p):
        store_bc(p)
        store_x(p)
        send_halo(p)

    def project(p, own_plane):
        complete(p, own_plane)
        product(p, 0, FIRST)
        store_first(p)

    def gates(p):
        product(p, FIRST, W)
        store_z(p)

    def taps_copy(k):
        slot = taps.at[quarter]
        return rcopy(slot, slot, cs.at[k], cr.at[quarter], head=base + (h + k + 1) % 4)

    def taps_wait(k):
        q = (h + k + 1) % 4
        rcopy(taps.at[q], taps.at[q], cs.at[k], cr.at[q], head=h).wait_recv()

    along(order[0], -1, True).start()
    along(order[0], 1, True).start()
    begin(order[0], True)
    for load in smalls + loads:
        load.start()
    for load in smalls:
        load.wait()
    taps[quarter, 0:4, 0:64] = cbc_v[...]
    for k in range(3):
        taps_copy(k).start()
    wt[W + 64:FIRST, :] = jnp.concatenate(
        [wdt_v[...].astype(F32), jnp.zeros((16 - HEADS, wt.shape[1]), F32)], axis=0).astype(BF16)
    halo_x[...] = jnp.zeros_like(halo_x)
    halo_b[...] = jnp.zeros_like(halo_b)
    for load in loads:
        load.wait()
    own.wait()

    arrive(1)
    near(order[0], True)
    arrive(2)
    last(order[0], True)
    near(order[1], False)
    project(order[0], True)
    arrive_early(2)
    near(order[2], False)
    last(order[1], False)
    arrive_early(1)
    arrive(3)
    gates(order[0])
    last(order[2], False)
    project(order[1], False)
    gates(order[1])
    near(order[3], False)
    project(order[2], False)
    pass_bc(order[0])
    arrive_early(3)
    last(order[3], False)
    pass_bc(order[1])
    pass_bc(order[2])
    complete_early(order[3])
    product(order[3], 0, FIRST, ((0, EARLY),))
    complete_late(order[3])
    product(order[3], 0, FIRST, ((EARLY, buf.shape[2] - EARLY),))
    store_first(order[3])

    def cols_of(b):
        return pl.ds(pl.multiple_of(slot_of(b // 2) * 256 + (b % 2) * 128, 128), 128)

    row = lax.broadcasted_iota(jnp.int32, (8, 128), 0)
    bias_col = jnp.zeros((8, 128), F32)
    rate_col = jnp.zeros((8, 128), F32)
    for k in range(HEADS):
        bias_col = jnp.where(row == k, bias[k], bias_col)
        rate_col = jnp.where(row == k, alog[k], rate_col)
    rate_col = jnp.exp(rate_col)
    upper = (lax.broadcasted_iota(jnp.int32, (128, 128), 0)
             <= lax.broadcasted_iota(jnp.int32, (128, 128), 1))
    parts = []
    for b in range(8):
        v = dt[0:8, cols_of(b)] + bias_col
        v = jnp.maximum(v, 0.0) + jnp.log1p(jnp.exp(-jnp.abs(v)))
        step[b * 8:(b + 1) * 8, :] = v
        parts.append(-v * rate_col)
    dec = jnp.concatenate(parts, axis=0)
    cum = jnp.dot(dec, upper.astype(F32), preferred_element_type=F32, precision=lax.Precision.HIGHEST)
    cums[...] = cum
    tot = jnp.broadcast_to(cum[:, 127:128], (64, 128))
    weight = step[...] * jnp.exp(tot - cum)
    cumt[...] = (cum - jnp.log(step[...])).T

    def mate_totals():
        return rcopy(tfin, tot_mate, ts, tr, seq=mate)

    run_t = jnp.zeros((8, 128), F32)
    first_t = run_t
    for k in range(4):
        if k:
            first_t = jnp.where(first_run == k, run_t, first_t)
            run_t = jnp.where(first_run == k, 0.0, run_t)
        for b in (2 * k, 2 * k + 1):
            offs[b] = run_t
            run_t = run_t + tot[b * 8:(b + 1) * 8, :]
    tfin[0] = jnp.where(first_run == 4, run_t, first_t)
    tfin[1] = jnp.where(first_run == 4, 0.0, run_t)
    mate_totals().start()

    lane = lax.broadcasted_iota(jnp.int32, (64, 128), 1)
    tapx = jnp.concatenate([cx_v[...], jnp.zeros((4, W), F32)], axis=0).T

    def conv_block(src, r0, taps, prev, b, dst, to):
        cur = src[r0:r0 + 64, cols_of(b)].astype(F32)
        total = taps[:, 3:4] * cur
        for k in range(1, 4):
            moved = pltpu.roll(jnp.where(lane >= 128 - k, prev, cur), k, 1)
            total = total + taps[:, 3 - k:4 - k] * moved
        dst[r0:r0 + 64, to] = silu(total).astype(BF16)
        return cur

    def conv(src, r0, taps, dst):
        prev = src[r0:r0 + 64, cols_of(0)].astype(F32)
        for b in range(1, 8):
            prev = conv_block(src, r0, taps, prev, b, dst, slice(b * 128, (b + 1) * 128))

    for k in range(HEADS):
        conv(pre, k * 64, tapx[k * 64:(k + 1) * 64], xc)
    pass_bc(order[3])
    gates(order[2])
    for k in range(3):
        taps_wait(k)
    tapb = [taps[q].T[0:64] for q in range(4)]
    for p in range(4):
        share_wait(p, 0)
        share_wait(p, 2)
    for q in range(4):
        conv(bcp, q * 64, tapb[q], bcf)

    def starts(i, b):
        to = pl.ds(pl.multiple_of(b * 128, 128), 128)
        for k in range(HEADS):
            conv_block(pre, k * 64, tapx[k * 64:(k + 1) * 64], hpad[i, k * 64:(k + 1) * 64, :], b, xc, to)
        for q in range(4):
            conv_block(bcp, q * 64, tapb[q], hpad[i, W + q * 64:W + (q + 1) * 64, :], b, bcf, to)

    halo_due = (jnp.logical_or(middle, x > 0), jnp.logical_and(ends, z != 1))
    hpad[0] = jnp.zeros((W + 256, 128), F32)
    for i in range(2):
        @pl.when(halo_due[i])
        def _():
            rcopy(halo_x.at[i], in_x.at[i], hxs.at[i], hxr.at[i], seq=s).wait_recv()
            hpad[i, 0:W, :] = lax.dot_general(in_x[i, :, 0:W], pick, TN, preferred_element_type=F32)
            for q in range(4):
                rcopy(halo_b.at[i], in_b.at[i, q], hbs.at[i, 0], hbr.at[i, q], seq=s).wait_recv()
                hpad[i, W + q * 64:W + q * 64 + 64, :] = lax.dot_general(
                    in_b[i, q, :, 0:64], pick, TN, preferred_element_type=F32)
            if i:
                starts(1, 2 * first_run)

    starts(0, 0)

    def rows(v, r):
        return jnp.concatenate(
            [jnp.broadcast_to(v[r + k:r + k + 1, :], (64, 128)) for k in range(HEADS)], axis=0)

    state = jnp.zeros((W, 128), F32)
    own_s[1] = state
    for k in range(4):
        if k:
            @pl.when(first_run == k)
            def _():
                own_s[0] = state

            state = jnp.where(first_run == k, 0.0, state)
        for b in (2 * k, 2 * k + 1):
            cols = slice(b * 128, (b + 1) * 128)
            sstart[b] = state
            xw = (xc[:, cols].astype(F32) * rows(weight, b * 8)).astype(BF16)
            fresh = lax.dot_general(xw, bcf[0:128, cols], NT, preferred_element_type=F32)
            state = state * rows(jnp.exp(tot[b * 8:(b + 1) * 8, :]), 0) + fresh

    @pl.when(first_run == 4)
    def _():
        own_s[0] = state

    @pl.when(first_run < 4)
    def _():
        own_s[1] = state

    def grown(v, t):
        return v * rows(jnp.exp(t), 0)

    mate_totals().wait_recv()
    head_t = jnp.where(ends, tfin[0], tot_mate[0])
    mid_t = jnp.where(ends, tot_mate[0], tfin[0])
    tail_t = jnp.where(ends, tfin[1], tot_mate[1])
    xfin[...] = (grown(own_s[0], jnp.where(ends, mid_t + tail_t, tail_t)) + own_s[1]).astype(BF16)
    xtot[...] = head_t + mid_t + tail_t
    for t in range(1, 4):
        @pl.when(x + t < 4)
        def _():
            rcopy(xfin, st_in.at[x], xs.at[t], xr.at[x], seq=s + 2 * t).start()
            rcopy(xtot, tot_in.at[x], vs.at[t], vr.at[x], seq=s + 2 * t).start()

    def mate_copy(i):
        return rcopy(sfin.at[i], st_mate.at[i], ss.at[i], sr.at[i], seq=mate)

    @pl.when(middle)
    def _():
        sfin[0] = own_s[0].astype(BF16)
        mate_copy(0).start()

    gates(order[3])
    inc[0] = jnp.zeros((W, 128), F32)
    for q in range(3):
        @pl.when(q < x)
        def _():
            rcopy(xfin, st_in.at[q], xs.at[0], xr.at[q], seq=s).wait_recv()
            rcopy(xtot, tot_in.at[q], vs.at[0], vr.at[q], seq=s).wait_recv()
            inc[0] = grown(inc[0], tot_in[q]) + st_in[q].astype(F32)

    carried = grown(inc[0], head_t)
    sfin[1] = jnp.where(ends, carried + own_s[0], inc[0]).astype(BF16)
    mate_copy(1).start()
    for b in range(8):
        cols = slice(b * 128, (b + 1) * 128)
        scores = lax.dot_general(bcf[0:128, cols], bcf[128:256, cols], TN, preferred_element_type=F32)
        scores = jnp.where(upper, scores, 0.0)
        for k in range(HEADS):
            r = b * 8 + k
            diff = cums[r:r + 1, :] - cumt[:, r:r + 1]
            mixing = jnp.exp(jnp.where(upper, diff, -jnp.inf)) * scores
            yin[k * 64:(k + 1) * 64, cols] = jnp.dot(
                xc[k * 64:(k + 1) * 64, cols], mixing.astype(BF16), preferred_element_type=F32)

    mate_copy(1).wait_recv()
    met = st_mate[1].astype(F32)
    inc[0] = jnp.where(ends, inc[0], carried) + met

    @pl.when(ends)
    def _():
        mate_copy(0).wait_recv()
        inc[1] = grown(grown(inc[0], head_t) + own_s[0], mid_t) + st_mate[0].astype(F32)

    skips = jnp.concatenate([jnp.full((64, 128), skip[k], F32) for k in range(HEADS)], axis=0)
    def send_out(dst):
        return rcopy(sb.at[dst], rbuf.at[h], as_.at[dst], ar.at[h], seq=owner(dst // 8), head=dst)

    for slot in (order[3], order[1], order[2], order[0]):
        for half in range(2):
            k = (slot - turn + 4) % 4
            b = 2 * k + half
            cols = pl.ds(pl.multiple_of(b * 128, 128), 128)
            run = jnp.where(first_run <= k, 1, 0)
            st = (sstart[b] + inc[run] * rows(jnp.exp(offs[b]), 0)).astype(BF16)
            yst = jnp.dot(st, bcf[128:256, cols], preferred_element_type=F32)
            near_t = jnp.exp(cums[pl.ds(pl.multiple_of(b * 8, 8), 8), :])
            yv = yin[:, cols] + yst * rows(near_t, 0) + skips * xc[:, cols].astype(F32)
            yv = yv.astype(BF16).astype(F32)
            gate = pre[W:BB, pl.ds(pl.multiple_of(slot * 256 + half * 128, 128), 128)]
            g = (yv * silu(gate.astype(F32))).T
            for i in range(4):
                dst = slot * 8 + 4 * half + i
                sb[dst, :, 0:W] = g[32 * i:32 * i + 16, :].astype(BF16)
                sb[dst, :, W:BB] = g[32 * i + 16:32 * i + 32, :].astype(BF16)
            for i in range(4):
                dst = slot * 8 + 4 * half + i

                @pl.when(dst != h)
                def _():
                    send_out(dst).start()

    keep = pltpu.make_async_copy(sb.at[h], rbuf.at[h], lsem.at[7])
    keep.start()

    def collect(k, _):
        src = (h + k) % 32
        rcopy(sb.at[src], rbuf.at[src], as_.at[src], ar.at[src], head=h).wait_recv()
        return 0

    lax.fori_loop(1, 32, collect, 0)

    keep.wait()
    for k in range(3):
        taps_copy(k).wait_send()
    for j in range(4):
        p = order[j]
        for sign in (-1, 1)[:2 if j == 0 else 1 if j == 1 else 0]:
            along(p, sign, j == 0).wait_send()
            for yy in (left, right, far):
                along_early(p, yy, sign).wait_send()
        for kind in range(4):
            ring(p, kind, j == 0).wait_send()
        twin(p, y, True, j == 0).wait_send()
        for yy in (left, right, far):
            twin(p, yy, j == 0).wait_send()
            if j:
                twin_early(p, yy).wait_send()
        for kind in range(3):
            share_copy(p, kind).wait_send()

    for i in range(2):
        @pl.when(halo_when[i])
        def _():
            for copy in halo_copies(i):
                copy.wait_send()

    mate_totals().wait_send()
    mate_copy(1).wait_send()

    @pl.when(middle)
    def _():
        mate_copy(0).wait_send()

    for t in range(1, 4):
        @pl.when(x + t < 4)
        def _():
            rcopy(xfin, st_in.at[x], xs.at[t], xr.at[x], seq=s).wait_send()
            rcopy(xtot, tot_in.at[x], vs.at[t], vr.at[x], seq=s).wait_send()

    def sent(k, _):
        dst = (h + k) % 32
        rcopy(sb.at[dst], rbuf.at[h], as_.at[dst], ar.at[h], head=h).wait_send()
        return 0

    lax.fori_loop(1, 32, sent, 0)


def norm_kernel(parts, gain, out, asm):
    for q in range(32):
        asm[0:16, q * W:(q + 1) * W] = parts[q, :, 0:W]
        asm[16:32, q * W:(q + 1) * W] = parts[q, :, W:BB]
    for g in range(5):
        v = asm[:, g * 2048:(g + 1) * 2048].astype(F32)
        scale = lax.rsqrt(jnp.mean(v * v, axis=1, keepdims=True) + 1e-5)
        for k in range(16):
            c0 = g * 16 + k
            out[:, c0 * 128:(c0 + 1) * 128] = (
                v[:, k * 128:(k + 1) * 128] * scale * gain[c0:c0 + 1, :]).astype(BF16)


def call(tok, wx, wz, wbc, wdt, cx, cbc, bias, alog, skip, gain):
    d = tok.shape[1]
    anywhere = pl.BlockSpec(memory_space=pl.ANY)
    vm = pl.BlockSpec(memory_space=pltpu.VMEM)
    sm = pl.BlockSpec(memory_space=pltpu.SMEM)
    dma = pltpu.SemaphoreType.DMA
    mem = pltpu.VMEM
    parts = pl.pallas_call(
        kernel,
        out_shape=jax.ShapeDtypeStruct((32, 16, BB), BF16),
        in_specs=[anywhere] * 7 + [sm] * 3,
        out_specs=anywhere,
        scratch_shapes=[
            mem((HEADS, d), BF16), mem((4, W), F32), mem((4, 64), F32),
            mem((32, 32, d), BF16), mem((BB + 80, d), BF16), mem((BB + 80, 256), F32),
            mem((BB, 1024), BF16), mem((16, 1024), F32), mem((256, 1024), BF16), mem((256, 1024), BF16),
            mem((2, 16, 384), BF16), mem((2, 16, 128), BF16), mem((2, 16, 384), BF16), mem((2, 4, 16, 128), BF16),
            mem((2, W + 256, 128), F32), mem((4, 8, 128), F32), mem((W, 1024), BF16),
            mem((64, 128), F32), mem((64, 128), F32), mem((128, 64), F32), mem((W, 1024), F32),
            mem((8, W, 128), F32), mem((8, 8, 128), F32), mem((2, W, 128), BF16), mem((2, 8, 128), F32),
            mem((2, W, 128), BF16), mem((2, 8, 128), F32), mem((2, W, 128), F32),
            mem((W, 128), BF16), mem((8, 128), F32),
            mem((3, W, 128), BF16), mem((3, 8, 128), F32), mem((2, W, 128), F32),
            mem((32, 16, BB), BF16),
            dma((8,)), dma((4, 2)), dma((4,)), dma((4, 4, 2)), dma((4, 4)),
            dma((4, 4)), dma((4, 4)), dma((4, 4)), dma((4, 4)), dma((4, 4)), dma((4, 4)),
            dma((4, 3)), dma((4, 3)), dma((3,)), dma((4,)), dma((2,)), dma((2,)), dma((2, 4)), dma((2, 4)),
            dma((2,)), dma((2,)), dma, dma, dma((4,)), dma((3,)), dma((4,)), dma((3,)),
            dma((32,)), dma((32,)),
        ],
        compiler_params=pltpu.CompilerParams(collective_id=0, has_side_effects=True,
                                             vmem_limit_bytes=60 * 2**20),
        name="mixer",
    )(tok, wx, wz, wbc, wdt, cx, cbc, bias, alog, skip)
    return pl.pallas_call(
        norm_kernel,
        out_shape=jax.ShapeDtypeStruct((32, 10240), BF16),
        in_specs=[vm, vm],
        out_specs=vm,
        scratch_shapes=[mem((32, 10240), BF16)],
        name="norm",
    )(parts, gain.reshape(80, 128))


def shards(tokens, wx, wz, wbc, wdt, cx, cbc, bias, alog, skip, gain):
    return call(tokens, wx.T, wz.T, wbc.T, wdt.T, cx, cbc, bias, alog, skip, gain)


def solution(mesh):
    cols = P(None, "head")
    placed = (P(("seq", "head"), None), cols, cols, cols, cols, cols, cols,
              P("head"), P("head"), P("head"), P())
    return jax.shard_map(
        shards, mesh=mesh, in_specs=placed, out_specs=P(("seq", "head"), None), check_vma=False
    )
```

```python
import jax
import jax.numpy as jnp
from jax import lax
from jax.experimental import pallas as pl
from jax.experimental.pallas import tpu as pltpu
from jax.sharding import PartitionSpec as P

MESH = pl.DeviceIdType.MESH
F32 = jnp.float32
BF16 = jnp.bfloat16
NT = (((1,), (1,)), ((), ()))
TN = (((0,), (0,)), ((), ()))
KC = 4096
EARLY = 3072
HEADS = 5
W = 320
BB = 2 * W
FIRST = W + 80
NSEQ = 8


def rcopy(src, dst, send, recv, **device):
    return pltpu.make_async_remote_copy(
        src_ref=src, dst_ref=dst, send_sem=send, recv_sem=recv,
        device_id=device, device_id_type=MESH,
    )


def silu(v):
    return v / (1.0 + jnp.exp(-v))


def kernel(tok, wx, wz, wbc, wdt, cx, cbc, bias, alog, skip, rbuf,
           wdt_v, cx_v, cbc_v, buf, wt, res, pre, dt, bcp, bcf, halo_x, halo_b, in_x, in_b, hpad, taps, xc,
           step, cums, cumt, yin, sstart, offs, sfin, tfin, st_mate, tot_mate, own_s, xfin, xtot, st_in, tot_in, inc, sb,
           lsem, zs, zr, es, er, ys, yr, ds, dr, fs, fr,
           bs, br, cs, cr, hxs, hxr, hbs, hbr, ss, sr, ts, tr, xs, xr, vs, vr, as_, ar):
    h = lax.axis_index("head")
    s = lax.axis_index("seq")
    z, y, c = h // 8, (h // 2) % 4, h % 2
    right, left, far = (y + 1) % 4, (y + 3) % 4, (y + 2) % 4
    sib = h + 1 - 2 * c
    across = h + 2 - 4 * (y % 2)
    base = (h // 4) * 4
    quarter = h % 4
    x, zh = s // 2, s % 2
    place = zh * 4 + z
    mate = s + 1 - 2 * zh
    ends = jnp.logical_or(place < 2, place >= 6)
    middle = jnp.logical_not(ends)
    first_run = jnp.where(ends, (place + 3) % 8, 4)
    turn = jnp.where(ends, 0, (place + 7) % 4)
    order = [z, (z + 1) % 4, (z + 3) % 4, (z + 2) % 4]

    def plane_in(slot):
        return (place + 7 + (slot - z + 5) % 4) % 8

    def owner(slot):
        return x * 2 + plane_in(slot) // 4

    def slot_of(k):
        return (turn + k) % 4

    def upward(dz):
        there = (place + dz + 8) % 8
        return dict(seq=x * 2 + there // 4, head=(there % 4) * 8 + y * 2 + c)

    def at(p, yy):
        return p * 8 + yy * 2 + c

    own = pltpu.make_async_copy(tok, buf.at[h], lsem.at[0])
    own.start()
    loads = [
        pltpu.make_async_copy(wx, wt.at[pl.ds(0, W)], lsem.at[1]),
        pltpu.make_async_copy(wz, wt.at[pl.ds(FIRST, W)], lsem.at[2]),
        pltpu.make_async_copy(wbc, wt.at[pl.ds(W, 64)], lsem.at[3]),
    ]
    smalls = [pltpu.make_async_copy(src, dst, lsem.at[4 + i])
              for i, (src, dst) in enumerate(((wdt, wdt_v), (cx, cx_v), (cbc, cbc_v)))]
    barrier = pltpu.get_barrier_semaphore()

    def signal(**device):
        pl.semaphore_signal(barrier, inc=1, device_id=device, device_id_type=MESH)

    for dz in (-1, 1, -2, 0):
        there = (place + dz + 8) % 8
        seq, first = x * 2 + there // 4, (there % 4) * 8
        for k in range(8):
            if dz:
                signal(seq=seq, head=first + k)
            else:
                @pl.when(first + k != h)
                def _():
                    signal(seq=seq, head=first + k)

    for k in range(1, 4):
        signal(seq=(s + 2 * k) % NSEQ)
    for k in range(4):
        signal(seq=mate, head=base + k)
    joined = jnp.logical_and(z == 1, middle)
    alone = jnp.logical_and(z == 1, ends)
    hand_on = jnp.logical_and(x < 3, jnp.logical_not(alone))
    next_seq = jnp.where(joined, mate + 2, s + 2)
    prev_seq = jnp.where(alone, mate - 2, s - 2)

    @pl.when(jnp.logical_and(x > 0, ends))
    def _():
        for k in range(4):
            signal(seq=prev_seq, head=base + k)

    hands_on = jnp.logical_and(hand_on, jnp.logical_or(ends, joined))
    pl.semaphore_wait(barrier, 31 + 3 + 4 + 4 * hands_on.astype(jnp.int32))
    early = pl.ds(0, EARLY)
    late = pl.ds(EARLY, buf.shape[2] - EARLY)

    def along(p, sign, own_plane):
        slot = buf.at[at(p, y)]
        return rcopy(tok if own_plane else slot, slot, zs.at[p, (sign + 1) // 2], zr.at[p], **upward(sign))

    def along_early(p, yy, sign):
        slot = buf.at[at(p, yy), :, early]
        return rcopy(slot, slot, es.at[p, yy, (sign + 1) // 2], er.at[p, yy], **upward(sign))

    def ring(p, kind, own_plane):
        cols = pl.ds(0, buf.shape[2]) if own_plane else late
        yy, rows, to = (
            (y, pl.ds(0, 32), right), (y, pl.ds(0, 32), left),
            (left, pl.ds(0, 16), right), (right, pl.ds(16, 16), left),
        )[kind]
        part = buf.at[at(p, yy), rows, cols]
        src = tok if own_plane and kind < 2 else part
        return rcopy(src, part, ys.at[p, kind], yr.at[p, kind], head=at(z, to))

    def ring_wait(p, kind, own_plane):
        cols = pl.ds(0, buf.shape[2]) if own_plane else late
        yy, rows = ((left, pl.ds(0, 32)), (right, pl.ds(0, 32)),
                    (far, pl.ds(0, 16)), (far, pl.ds(16, 16)))[kind]
        part = buf.at[at(p, yy), rows, cols]
        rcopy(part, part, ys.at[p, kind], yr.at[p, kind], head=h).wait_recv()

    def twin(p, yy, whole, mine=False):
        slot = buf.at[at(p, yy)] if whole else buf.at[at(p, yy), :, late]
        return rcopy(tok if mine else slot, slot, ds.at[p, yy], dr.at[p, yy], head=sib)

    def twin_wait(p, yy, whole):
        slot = buf.at[p * 8 + yy * 2 + 1 - c]
        slot = slot if whole else slot.at[:, late]
        rcopy(slot, slot, ds.at[p, yy], dr.at[p, yy], head=h).wait_recv()

    def twin_early(p, yy):
        slot = buf.at[at(p, yy), :, early]
        return rcopy(slot, slot, fs.at[p, yy], fr.at[p, yy], head=sib)

    def twin_early_wait(p, yy):
        slot = buf.at[p * 8 + yy * 2 + 1 - c, :, early]
        rcopy(slot, slot, fs.at[p, yy], fr.at[p, yy], head=h).wait_recv()

    def begin(p, own_plane):
        ring(p, 0, own_plane).start()
        ring(p, 1, own_plane).start()
        twin(p, y, True, own_plane).start()

    def arrive(j):
        p = order[j]
        slot = buf.at[at(p, y)]
        rcopy(slot, slot, zs.at[p, 0], zr.at[p], head=h).wait_recv()
        if j == 1:
            along(p, -1, False).start()
        begin(p, False)

    def arrive_early(j):
        p = order[j]
        for yy in (left, right, far):
            slot = buf.at[at(p, yy), :, early]
            rcopy(slot, slot, es.at[p, yy, 0], er.at[p, yy], head=h).wait_recv()
            if j == 1:
                along_early(p, yy, -1).start()
            twin_early(p, yy).start()

    def near(p, own_plane):
        ring_wait(p, 0, own_plane)
        ring(p, 2, own_plane).start()
        ring_wait(p, 1, own_plane)
        ring(p, 3, own_plane).start()
        for yy in (left, right):
            twin(p, yy, own_plane).start()
            if own_plane:
                along_early(p, yy, -1).start()
                along_early(p, yy, 1).start()

    def last(p, own_plane):
        ring_wait(p, 2, own_plane)
        ring_wait(p, 3, own_plane)
        twin(p, far, own_plane).start()
        if own_plane:
            along_early(p, far, -1).start()
            along_early(p, far, 1).start()

    def complete_early(p):
        twin_wait(p, y, True)
        for yy in (left, right, far):
            twin_early_wait(p, yy)

    def complete_late(p):
        for yy in (left, right, far):
            twin_wait(p, yy, False)

    def complete(p, own_plane):
        if own_plane:
            for yy in (y, left, right, far):
                twin_wait(p, yy, True)
        else:
            complete_early(p)
            complete_late(p)

    def product(p, r0, n, parts=((0, KC), (KC, KC))):
        for k0, count in parts:
            a = buf[pl.ds(p * 8, 8), :, k0:k0 + count].reshape(256, count)
            part = lax.dot_general(wt[r0:r0 + n, k0:k0 + count], a, NT, preferred_element_type=F32)
            res[r0:r0 + n] = part if k0 == 0 else res[r0:r0 + n] + part

    def span_of(p):
        return pl.ds(pl.multiple_of(p * 256, 256), 256)

    def quarter_rows(q):
        return pl.ds(pl.multiple_of(q * 64, 64), 64)

    q_sib = quarter + 1 - 2 * c
    q_across = quarter + 2 - 4 * (y % 2)
    q_other = q_across + 1 - 2 * c

    def share_copy(p, kind):
        q = (quarter, quarter, q_across)[kind]
        part = bcp.at[quarter_rows(q), span_of(p)]
        return rcopy(part, part, bs.at[p, kind], br.at[p, kind], head=(sib, across, sib)[kind])

    def share_wait(p, kind):
        q = (q_sib, q_across, q_other)[kind]
        part = bcp.at[quarter_rows(q), span_of(p)]
        rcopy(part, part, bs.at[p, kind], br.at[p, kind], head=h).wait_recv()

    def store_bc(p):
        span = span_of(p)
        bcp[quarter_rows(quarter), span] = res[W:W + 64].astype(BF16)
        dt[:, span] = res[W + 64:FIRST]
        share_copy(p, 0).start()
        share_copy(p, 1).start()

    def pass_bc(p):
        share_wait(p, 1)
        share_copy(p, 2).start()

    def store_x(p):
        pre[0:W, span_of(p)] = res[0:W].astype(BF16)

    def store_z(p):
        pre[W:BB, span_of(p)] = res[FIRST:FIRST + W].astype(BF16)

    pick = (lax.broadcasted_iota(jnp.int32, (16, 128), 1)
            == lax.broadcasted_iota(jnp.int32, (16, 128), 0) + 112).astype(BF16)

    def halo_copies(i):
        if i == 0:
            to, slot = jnp.where(joined, next_seq, mate), jnp.where(jnp.logical_or(ends, joined), 0, 1)
        else:
            to, slot = next_seq, 0
        yield rcopy(halo_x.at[i], in_x.at[slot], hxs.at[i], hxr.at[slot], seq=to)
        for k in range(4):
            yield rcopy(halo_b.at[i], in_b.at[slot, quarter], hbs.at[i, k], hbr.at[slot, quarter],
                        seq=to, head=base + k)

    halo_when = (jnp.logical_or(jnp.logical_not(joined), x < 3), jnp.logical_and(ends, hand_on))
    halo_slot = (order[3], 3)

    def send_halo(p):
        for i in range(2):
            @pl.when(jnp.logical_and(p == halo_slot[i], halo_when[i]))
            def _():
                tail = pl.ds(pl.multiple_of(p * 256 + 128, 128), 128)
                halo_x[i, :, 0:W] = lax.dot_general(
                    pick, pre[0:W, tail], NT, preferred_element_type=F32).astype(BF16)
                halo_b[i, :, 0:64] = lax.dot_general(
                    pick, bcp[quarter_rows(quarter), tail], NT, preferred_element_type=F32).astype(BF16)
                for copy in halo_copies(i):
                    copy.start()

    def store_first(p):
        store_bc(p)
        store_x(p)
        send_halo(p)

    def project(p, own_plane):
        complete(p, own_plane)
        product(p, 0, FIRST)
        store_first(p)

    def gates(p):
        product(p, FIRST, W)
        store_z(p)

    def taps_copy(k):
        slot = taps.at[quarter]
        return rcopy(slot, slot, cs.at[k], cr.at[quarter], head=base + (h + k + 1) % 4)

    def taps_wait(k):
        q = (h + k + 1) % 4
        rcopy(taps.at[q], taps.at[q], cs.at[k], cr.at[q], head=h).wait_recv()

    along(order[0], -1, True).start()
    along(order[0], 1, True).start()
    begin(order[0], True)
    for load in smalls + loads:
        load.start()
    for load in smalls:
        load.wait()
    taps[quarter, 0:4, 0:64] = cbc_v[...]
    for k in range(3):
        taps_copy(k).start()
    wt[W + 64:FIRST, :] = jnp.concatenate(
        [wdt_v[...].astype(F32), jnp.zeros((16 - HEADS, wt.shape[1]), F32)], axis=0).astype(BF16)
    halo_x[...] = jnp.zeros_like(halo_x)
    halo_b[...] = jnp.zeros_like(halo_b)
    for load in loads:
        load.wait()
    own.wait()

    arrive(1)
    near(order[0], True)
    arrive(2)
    last(order[0], True)
    near(order[1], False)
    project(order[0], True)
    arrive_early(2)
    near(order[2], False)
    last(order[1], False)
    arrive_early(1)
    arrive(3)
    gates(order[0])
    last(order[2], False)
    project(order[1], False)
    gates(order[1])
    near(order[3], False)
    project(order[2], False)
    pass_bc(order[0])
    arrive_early(3)
    last(order[3], False)
    pass_bc(order[1])
    pass_bc(order[2])
    complete_early(order[3])
    product(order[3], 0, FIRST, ((0, EARLY),))
    complete_late(order[3])
    product(order[3], 0, FIRST, ((EARLY, buf.shape[2] - EARLY),))
    store_first(order[3])

    def cols_of(b):
        return pl.ds(pl.multiple_of(slot_of(b // 2) * 256 + (b % 2) * 128, 128), 128)

    row = lax.broadcasted_iota(jnp.int32, (8, 128), 0)
    bias_col = jnp.zeros((8, 128), F32)
    rate_col = jnp.zeros((8, 128), F32)
    for k in range(HEADS):
        bias_col = jnp.where(row == k, bias[k], bias_col)
        rate_col = jnp.where(row == k, alog[k], rate_col)
    rate_col = jnp.exp(rate_col)
    upper = (lax.broadcasted_iota(jnp.int32, (128, 128), 0)
             <= lax.broadcasted_iota(jnp.int32, (128, 128), 1))
    parts = []
    for b in range(8):
        v = dt[0:8, cols_of(b)] + bias_col
        v = jnp.maximum(v, 0.0) + jnp.log1p(jnp.exp(-jnp.abs(v)))
        step[b * 8:(b + 1) * 8, :] = v
        parts.append(-v * rate_col)
    dec = jnp.concatenate(parts, axis=0)
    cum = jnp.dot(dec, upper.astype(F32), preferred_element_type=F32, precision=lax.Precision.HIGHEST)
    cums[...] = cum
    tot = jnp.broadcast_to(cum[:, 127:128], (64, 128))
    weight = step[...] * jnp.exp(tot - cum)
    cumt[...] = (cum - jnp.log(step[...])).T

    def mate_totals():
        return rcopy(tfin, tot_mate, ts, tr, seq=mate)

    run_t = jnp.zeros((8, 128), F32)
    first_t = run_t
    for k in range(4):
        if k:
            first_t = jnp.where(first_run == k, run_t, first_t)
            run_t = jnp.where(first_run == k, 0.0, run_t)
        for b in (2 * k, 2 * k + 1):
            offs[b] = run_t
            run_t = run_t + tot[b * 8:(b + 1) * 8, :]
    tfin[0] = jnp.where(first_run == 4, run_t, first_t)
    tfin[1] = jnp.where(first_run == 4, 0.0, run_t)
    mate_totals().start()

    lane = lax.broadcasted_iota(jnp.int32, (64, 128), 1)
    tapx = jnp.concatenate([cx_v[...], jnp.zeros((4, W), F32)], axis=0).T

    def conv_block(src, r0, taps, prev, b, dst, to):
        cur = src[r0:r0 + 64, cols_of(b)].astype(F32)
        total = taps[:, 3:4] * cur
        for k in range(1, 4):
            moved = pltpu.roll(jnp.where(lane >= 128 - k, prev, cur), k, 1)
            total = total + taps[:, 3 - k:4 - k] * moved
        dst[r0:r0 + 64, to] = silu(total).astype(BF16)
        return cur

    def conv(src, r0, taps, dst):
        prev = src[r0:r0 + 64, cols_of(0)].astype(F32)
        for b in range(1, 8):
            prev = conv_block(src, r0, taps, prev, b, dst, slice(b * 128, (b + 1) * 128))

    for k in range(HEADS):
        conv(pre, k * 64, tapx[k * 64:(k + 1) * 64], xc)
    pass_bc(order[3])
    gates(order[2])
    for k in range(3):
        taps_wait(k)
    tapb = [taps[q].T[0:64] for q in range(4)]
    for p in range(4):
        share_wait(p, 0)
        share_wait(p, 2)
    for q in range(4):
        conv(bcp, q * 64, tapb[q], bcf)

    def starts(i, b):
        to = pl.ds(pl.multiple_of(b * 128, 128), 128)
        for k in range(HEADS):
            conv_block(pre, k * 64, tapx[k * 64:(k + 1) * 64], hpad[i, k * 64:(k + 1) * 64, :], b, xc, to)
        for q in range(4):
            conv_block(bcp, q * 64, tapb[q], hpad[i, W + q * 64:W + (q + 1) * 64, :], b, bcf, to)

    halo_due = (jnp.logical_or(middle, x > 0), jnp.logical_and(ends, z != 1))
    hpad[0] = jnp.zeros((W + 256, 128), F32)
    for i in range(2):
        @pl.when(halo_due[i])
        def _():
            rcopy(halo_x.at[i], in_x.at[i], hxs.at[i], hxr.at[i], seq=s).wait_recv()
            hpad[i, 0:W, :] = lax.dot_general(in_x[i, :, 0:W], pick, TN, preferred_element_type=F32)
            for q in range(4):
                rcopy(halo_b.at[i], in_b.at[i, q], hbs.at[i, 0], hbr.at[i, q], seq=s).wait_recv()
                hpad[i, W + q * 64:W + q * 64 + 64, :] = lax.dot_general(
                    in_b[i, q, :, 0:64], pick, TN, preferred_element_type=F32)
            if i:
                starts(1, 2 * first_run)

    starts(0, 0)

    def rows(v, r):
        return jnp.concatenate(
            [jnp.broadcast_to(v[r + k:r + k + 1, :], (64, 128)) for k in range(HEADS)], axis=0)

    state = jnp.zeros((W, 128), F32)
    own_s[1] = state
    for k in range(4):
        if k:
            @pl.when(first_run == k)
            def _():
                own_s[0] = state

            state = jnp.where(first_run == k, 0.0, state)
        for b in (2 * k, 2 * k + 1):
            cols = slice(b * 128, (b + 1) * 128)
            sstart[b] = state
            xw = (xc[:, cols].astype(F32) * rows(weight, b * 8)).astype(BF16)
            fresh = lax.dot_general(xw, bcf[0:128, cols], NT, preferred_element_type=F32)
            state = state * rows(jnp.exp(tot[b * 8:(b + 1) * 8, :]), 0) + fresh

    @pl.when(first_run == 4)
    def _():
        own_s[0] = state

    @pl.when(first_run < 4)
    def _():
        own_s[1] = state

    def grown(v, t):
        return v * rows(jnp.exp(t), 0)

    mate_totals().wait_recv()
    head_t = jnp.where(ends, tfin[0], tot_mate[0])
    mid_t = jnp.where(ends, tot_mate[0], tfin[0])
    tail_t = jnp.where(ends, tfin[1], tot_mate[1])
    xfin[...] = (grown(own_s[0], jnp.where(ends, mid_t + tail_t, tail_t)) + own_s[1]).astype(BF16)
    xtot[...] = head_t + mid_t + tail_t
    for t in range(1, 4):
        @pl.when(x + t < 4)
        def _():
            rcopy(xfin, st_in.at[x], xs.at[t], xr.at[x], seq=s + 2 * t).start()
            rcopy(xtot, tot_in.at[x], vs.at[t], vr.at[x], seq=s + 2 * t).start()

    def mate_copy(i):
        return rcopy(sfin.at[i], st_mate.at[i], ss.at[i], sr.at[i], seq=mate)

    @pl.when(middle)
    def _():
        sfin[0] = own_s[0].astype(BF16)
        mate_copy(0).start()

    gates(order[3])
    inc[0] = jnp.zeros((W, 128), F32)
    for q in range(3):
        @pl.when(q < x)
        def _():
            rcopy(xfin, st_in.at[q], xs.at[0], xr.at[q], seq=s).wait_recv()
            rcopy(xtot, tot_in.at[q], vs.at[0], vr.at[q], seq=s).wait_recv()
            inc[0] = grown(inc[0], tot_in[q]) + st_in[q].astype(F32)

    carried = grown(inc[0], head_t)
    sfin[1] = jnp.where(ends, carried + own_s[0], inc[0]).astype(BF16)
    mate_copy(1).start()
    for b in range(8):
        cols = slice(b * 128, (b + 1) * 128)
        scores = lax.dot_general(bcf[0:128, cols], bcf[128:256, cols], TN, preferred_element_type=F32)
        scores = jnp.where(upper, scores, 0.0)
        for k in range(HEADS):
            r = b * 8 + k
            diff = cums[r:r + 1, :] - cumt[:, r:r + 1]
            mixing = jnp.exp(jnp.where(upper, diff, -jnp.inf)) * scores
            yin[k * 64:(k + 1) * 64, cols] = jnp.dot(
                xc[k * 64:(k + 1) * 64, cols], mixing.astype(BF16), preferred_element_type=F32)

    for k in range(3):
        taps_copy(k).wait_send()
    for j in range(4):
        p = order[j]
        for sign in (-1, 1)[:2 if j == 0 else 1 if j == 1 else 0]:
            along(p, sign, j == 0).wait_send()
            for yy in (left, right, far):
                along_early(p, yy, sign).wait_send()
        for kind in range(4):
            ring(p, kind, j == 0).wait_send()
        twin(p, y, True, j == 0).wait_send()
        for yy in (left, right, far):
            twin(p, yy, j == 0).wait_send()
            if j:
                twin_early(p, yy).wait_send()
        for kind in range(3):
            share_copy(p, kind).wait_send()

    for i in range(2):
        @pl.when(halo_when[i])
        def _():
            for copy in halo_copies(i):
                copy.wait_send()

    mate_totals().wait_send()
    mate_copy(1).wait_send()

    @pl.when(middle)
    def _():
        mate_copy(0).wait_send()

    for t in range(1, 4):
        @pl.when(x + t < 4)
        def _():
            rcopy(xfin, st_in.at[x], xs.at[t], xr.at[x], seq=s).wait_send()
            rcopy(xtot, tot_in.at[x], vs.at[t], vr.at[x], seq=s).wait_send()

    mate_copy(1).wait_recv()
    met = st_mate[1].astype(F32)
    inc[0] = jnp.where(ends, inc[0], carried) + met

    @pl.when(ends)
    def _():
        mate_copy(0).wait_recv()
        inc[1] = grown(grown(inc[0], head_t) + own_s[0], mid_t) + st_mate[0].astype(F32)

    skips = jnp.concatenate([jnp.full((64, 128), skip[k], F32) for k in range(HEADS)], axis=0)
    def send_out(dst):
        return rcopy(sb.at[dst], rbuf.at[h], as_, ar, seq=owner(dst // 8), head=dst)

    for slot in (order[3], order[1], order[2], order[0]):
        for half in range(2):
            k = (slot - turn + 4) % 4
            b = 2 * k + half
            cols = pl.ds(pl.multiple_of(b * 128, 128), 128)
            run = jnp.where(first_run <= k, 1, 0)
            st = (sstart[b] + inc[run] * rows(jnp.exp(offs[b]), 0)).astype(BF16)
            yst = jnp.dot(st, bcf[128:256, cols], preferred_element_type=F32)
            near_t = jnp.exp(cums[pl.ds(pl.multiple_of(b * 8, 8), 8), :])
            yv = yin[:, cols] + yst * rows(near_t, 0) + skips * xc[:, cols].astype(F32)
            yv = yv.astype(BF16).astype(F32)
            gate = pre[W:BB, pl.ds(pl.multiple_of(slot * 256 + half * 128, 128), 128)]
            g = (yv * silu(gate.astype(F32))).T
            for i in range(4):
                dst = slot * 8 + 4 * half + i
                sb[dst, :, 0:W] = g[32 * i:32 * i + 16, :].astype(BF16)
                sb[dst, :, W:BB] = g[32 * i + 16:32 * i + 32, :].astype(BF16)
            for i in range(4):
                dst = slot * 8 + 4 * half + i

                @pl.when(dst != h)
                def _():
                    send_out(dst).start()

    keep = pltpu.make_async_copy(sb.at[h], rbuf.at[h], lsem.at[7])
    keep.start()

    everyone = rcopy(sb.at[pl.ds(0, 31)], rbuf.at[pl.ds(0, 31)], as_, ar, head=h)
    everyone.wait_send()
    everyone.wait_recv()
    keep.wait()


def norm_kernel(parts, gain, out, asm):
    for q in range(32):
        asm[0:16, q * W:(q + 1) * W] = parts[q, :, 0:W]
        asm[16:32, q * W:(q + 1) * W] = parts[q, :, W:BB]
    for g in range(5):
        v = asm[:, g * 2048:(g + 1) * 2048].astype(F32)
        scale = lax.rsqrt(jnp.mean(v * v, axis=1, keepdims=True) + 1e-5)
        for k in range(16):
            c0 = g * 16 + k
            out[:, c0 * 128:(c0 + 1) * 128] = (
                v[:, k * 128:(k + 1) * 128] * scale * gain[c0:c0 + 1, :]).astype(BF16)


def call(tok, wx, wz, wbc, wdt, cx, cbc, bias, alog, skip, gain):
    d = tok.shape[1]
    anywhere = pl.BlockSpec(memory_space=pl.ANY)
    vm = pl.BlockSpec(memory_space=pltpu.VMEM)
    sm = pl.BlockSpec(memory_space=pltpu.SMEM)
    dma = pltpu.SemaphoreType.DMA
    mem = pltpu.VMEM
    parts = pl.pallas_call(
        kernel,
        out_shape=jax.ShapeDtypeStruct((32, 16, BB), BF16),
        in_specs=[anywhere] * 7 + [sm] * 3,
        out_specs=anywhere,
        scratch_shapes=[
            mem((HEADS, d), BF16), mem((4, W), F32), mem((4, 64), F32),
            mem((32, 32, d), BF16), mem((BB + 80, d), BF16), mem((BB + 80, 256), F32),
            mem((BB, 1024), BF16), mem((16, 1024), F32), mem((256, 1024), BF16), mem((256, 1024), BF16),
            mem((2, 16, 384), BF16), mem((2, 16, 128), BF16), mem((2, 16, 384), BF16), mem((2, 4, 16, 128), BF16),
            mem((2, W + 256, 128), F32), mem((4, 8, 128), F32), mem((W, 1024), BF16),
            mem((64, 128), F32), mem((64, 128), F32), mem((128, 64), F32), mem((W, 1024), F32),
            mem((8, W, 128), F32), mem((8, 8, 128), F32), mem((2, W, 128), BF16), mem((2, 8, 128), F32),
            mem((2, W, 128), BF16), mem((2, 8, 128), F32), mem((2, W, 128), F32),
            mem((W, 128), BF16), mem((8, 128), F32),
            mem((3, W, 128), BF16), mem((3, 8, 128), F32), mem((2, W, 128), F32),
            mem((32, 16, BB), BF16),
            dma((8,)), dma((4, 2)), dma((4,)), dma((4, 4, 2)), dma((4, 4)),
            dma((4, 4)), dma((4, 4)), dma((4, 4)), dma((4, 4)), dma((4, 4)), dma((4, 4)),
            dma((4, 3)), dma((4, 3)), dma((3,)), dma((4,)), dma((2,)), dma((2,)), dma((2, 4)), dma((2, 4)),
            dma((2,)), dma((2,)), dma, dma, dma((4,)), dma((3,)), dma((4,)), dma((3,)),
            dma, dma,
        ],
        compiler_params=pltpu.CompilerParams(collective_id=0, has_side_effects=True,
                                             vmem_limit_bytes=60 * 2**20),
        name="mixer",
    )(tok, wx, wz, wbc, wdt, cx, cbc, bias, alog, skip)
    return pl.pallas_call(
        norm_kernel,
        out_shape=jax.ShapeDtypeStruct((32, 10240), BF16),
        in_specs=[vm, vm],
        out_specs=vm,
        scratch_shapes=[mem((32, 10240), BF16)],
        name="norm",
    )(parts, gain.reshape(80, 128))


def shards(tokens, wx, wz, wbc, wdt, cx, cbc, bias, alog, skip, gain):
    return call(tokens, wx.T, wz.T, wbc.T, wdt.T, cx, cbc, bias, alog, skip, gain)


def solution(mesh):
    cols = P(None, "head")
    placed = (P(("seq", "head"), None), cols, cols, cols, cols, cols, cols,
              P("head"), P("head"), P("head"), P())
    return jax.shard_map(
        shards, mesh=mesh, in_specs=placed, out_specs=P(("seq", "head"), None), check_vma=False
    )
```

```python
import jax
import jax.numpy as jnp
from jax import lax
from jax.experimental import pallas as pl
from jax.experimental.pallas import tpu as pltpu
from jax.sharding import PartitionSpec as P

MESH = pl.DeviceIdType.MESH
F32 = jnp.float32
BF16 = jnp.bfloat16
NT = (((1,), (1,)), ((), ()))
TN = (((0,), (0,)), ((), ()))
KC = 4096
EARLY = 3072
HEADS = 5
W = 320
BB = 2 * W
FIRST = W + 80
NSEQ = 8


def rcopy(src, dst, send, recv, **device):
    return pltpu.make_async_remote_copy(
        src_ref=src, dst_ref=dst, send_sem=send, recv_sem=recv,
        device_id=device, device_id_type=MESH,
    )


def silu(v):
    return v / (1.0 + jnp.exp(-v))


def kernel(tok, wx, wz, wbc, wdt, cx, cbc, bias, alog, skip, rbuf,
           wdt_v, cx_v, cbc_v, buf, wt, res, pre, dt, bcp, bcf, halo_x, halo_b, in_x, in_b, hpad, taps, xc,
           step, cums, cumt, yin, sstart, offs, sfin, tfin, st_mate, tot_mate, own_s, xfin, xtot, st_in, tot_in, inc, sb,
           lsem, zs, zr, es, er, ys, yr, ds, dr, fs, fr,
           bs, br, cs, cr, hxs, hxr, hbs, hbr, ss, sr, ts, tr, xs, xr, vs, vr, as_, ar):
    h = lax.axis_index("head")
    s = lax.axis_index("seq")
    z, y, c = h // 8, (h // 2) % 4, h % 2
    right, left, far = (y + 1) % 4, (y + 3) % 4, (y + 2) % 4
    sib = h + 1 - 2 * c
    across = h + 2 - 4 * (y % 2)
    base = (h // 4) * 4
    quarter = h % 4
    x, zh = s // 2, s % 2
    place = zh * 4 + z
    mate = s + 1 - 2 * zh
    ends = jnp.logical_or(place < 2, place >= 6)
    middle = jnp.logical_not(ends)
    first_run = jnp.where(ends, (place + 3) % 8, 4)
    turn = jnp.where(ends, 0, (place + 7) % 4)
    order = [z, (z + 1) % 4, (z + 3) % 4, (z + 2) % 4]

    def plane_in(slot):
        return (place + 7 + (slot - z + 5) % 4) % 8

    def owner(slot):
        return x * 2 + plane_in(slot) // 4

    def slot_of(k):
        return (turn + k) % 4

    def upward(dz):
        there = (place + dz + 8) % 8
        return dict(seq=x * 2 + there // 4, head=(there % 4) * 8 + y * 2 + c)

    def at(p, yy):
        return p * 8 + yy * 2 + c

    own = pltpu.make_async_copy(tok, buf.at[h], lsem.at[0])
    own.start()
    loads = [
        pltpu.make_async_copy(wx, wt.at[pl.ds(0, W)], lsem.at[1]),
        pltpu.make_async_copy(wz, wt.at[pl.ds(FIRST, W)], lsem.at[2]),
        pltpu.make_async_copy(wbc, wt.at[pl.ds(W, 64)], lsem.at[3]),
    ]
    smalls = [pltpu.make_async_copy(src, dst, lsem.at[4 + i])
              for i, (src, dst) in enumerate(((wdt, wdt_v), (cx, cx_v), (cbc, cbc_v)))]
    barrier = pltpu.get_barrier_semaphore()

    def signal(**device):
        pl.semaphore_signal(barrier, inc=1, device_id=device, device_id_type=MESH)

    for dz in (-1, 1, -2, 0):
        there = (place + dz + 8) % 8
        seq, first = x * 2 + there // 4, (there % 4) * 8
        for k in range(8):
            if dz:
                signal(seq=seq, head=first + k)
            else:
                @pl.when(first + k != h)
                def _():
                    signal(seq=seq, head=first + k)

    for k in range(1, 4):
        signal(seq=(s + 2 * k) % NSEQ)
    for k in range(4):
        signal(seq=mate, head=base + k)
    joined = jnp.logical_and(z == 1, middle)
    alone = jnp.logical_and(z == 1, ends)
    hand_on = jnp.logical_and(x < 3, jnp.logical_not(alone))
    next_seq = jnp.where(joined, mate + 2, s + 2)
    prev_seq = jnp.where(alone, mate - 2, s - 2)

    @pl.when(jnp.logical_and(x > 0, ends))
    def _():
        for k in range(4):
            signal(seq=prev_seq, head=base + k)

    hands_on = jnp.logical_and(hand_on, jnp.logical_or(ends, joined))
    pl.semaphore_wait(barrier, 31 + 3 + 4 + 4 * hands_on.astype(jnp.int32))
    early = pl.ds(0, EARLY)
    late = pl.ds(EARLY, buf.shape[2] - EARLY)

    def along(p, sign, own_plane):
        slot = buf.at[at(p, y)]
        return rcopy(tok if own_plane else slot, slot, zs.at[p, (sign + 1) // 2], zr.at[p], **upward(sign))

    def along_early(p, yy, sign):
        slot = buf.at[at(p, yy), :, early]
        return rcopy(slot, slot, es.at[p, yy, (sign + 1) // 2], er.at[p, yy], **upward(sign))

    def ring(p, kind, own_plane):
        cols = pl.ds(0, buf.shape[2]) if own_plane else late
        yy, rows, to = (
            (y, pl.ds(0, 32), right), (y, pl.ds(0, 32), left),
            (left, pl.ds(0, 16), right), (right, pl.ds(16, 16), left),
        )[kind]
        part = buf.at[at(p, yy), rows, cols]
        src = tok if own_plane and kind < 2 else part
        return rcopy(src, part, ys.at[p, kind], yr.at[p, kind], head=at(z, to))

    def ring_wait(p, kind, own_plane):
        cols = pl.ds(0, buf.shape[2]) if own_plane else late
        yy, rows = ((left, pl.ds(0, 32)), (right, pl.ds(0, 32)),
                    (far, pl.ds(0, 16)), (far, pl.ds(16, 16)))[kind]
        part = buf.at[at(p, yy), rows, cols]
        rcopy(part, part, ys.at[p, kind], yr.at[p, kind], head=h).wait_recv()

    def twin(p, yy, whole, mine=False):
        slot = buf.at[at(p, yy)] if whole else buf.at[at(p, yy), :, late]
        return rcopy(tok if mine else slot, slot, ds.at[p, yy], dr.at[p, yy], head=sib)

    def twin_wait(p, yy, whole):
        slot = buf.at[p * 8 + yy * 2 + 1 - c]
        slot = slot if whole else slot.at[:, late]
        rcopy(slot, slot, ds.at[p, yy], dr.at[p, yy], head=h).wait_recv()

    def twin_early(p, yy):
        slot = buf.at[at(p, yy), :, early]
        return rcopy(slot, slot, fs.at[p, yy], fr.at[p, yy], head=sib)

    def twin_early_wait(p, yy):
        slot = buf.at[p * 8 + yy * 2 + 1 - c, :, early]
        rcopy(slot, slot, fs.at[p, yy], fr.at[p, yy], head=h).wait_recv()

    def begin(p, own_plane):
        ring(p, 0, own_plane).start()
        ring(p, 1, own_plane).start()
        twin(p, y, True, own_plane).start()

    def arrive(j):
        p = order[j]
        slot = buf.at[at(p, y)]
        rcopy(slot, slot, zs.at[p, 0], zr.at[p], head=h).wait_recv()
        if j == 1:
            along(p, -1, False).start()
        begin(p, False)

    def arrive_early(j):
        p = order[j]
        for yy in (left, right, far):
            slot = buf.at[at(p, yy), :, early]
            rcopy(slot, slot, es.at[p, yy, 0], er.at[p, yy], head=h).wait_recv()
            if j == 1:
                along_early(p, yy, -1).start()
            twin_early(p, yy).start()

    def near(p, own_plane):
        ring_wait(p, 0, own_plane)
        ring(p, 2, own_plane).start()
        ring_wait(p, 1, own_plane)
        ring(p, 3, own_plane).start()
        for yy in (left, right):
            twin(p, yy, own_plane).start()
            if own_plane:
                along_early(p, yy, -1).start()
                along_early(p, yy, 1).start()

    def last(p, own_plane):
        ring_wait(p, 2, own_plane)
        ring_wait(p, 3, own_plane)
        twin(p, far, own_plane).start()
        if own_plane:
            along_early(p, far, -1).start()
            along_early(p, far, 1).start()

    def complete_early(p):
        twin_wait(p, y, True)
        for yy in (left, right, far):
            twin_early_wait(p, yy)

    def complete_late(p):
        for yy in (left, right, far):
            twin_wait(p, yy, False)

    def complete(p, own_plane):
        if own_plane:
            for yy in (y, left, right, far):
                twin_wait(p, yy, True)
        else:
            complete_early(p)
            complete_late(p)

    def product(p, r0, n, parts=((0, KC), (KC, KC))):
        for k0, count in parts:
            a = buf[pl.ds(p * 8, 8), :, k0:k0 + count].reshape(256, count)
            part = lax.dot_general(wt[r0:r0 + n, k0:k0 + count], a, NT, preferred_element_type=F32)
            res[r0:r0 + n] = part if k0 == 0 else res[r0:r0 + n] + part

    def span_of(p):
        return pl.ds(pl.multiple_of(p * 256, 256), 256)

    def quarter_rows(q):
        return pl.ds(pl.multiple_of(q * 64, 64), 64)

    q_sib = quarter + 1 - 2 * c
    q_across = quarter + 2 - 4 * (y % 2)
    q_other = q_across + 1 - 2 * c

    def share_copy(p, kind):
        q = (quarter, quarter, q_across)[kind]
        part = bcp.at[quarter_rows(q), span_of(p)]
        return rcopy(part, part, bs.at[p, kind], br.at[p, kind], head=(sib, across, sib)[kind])

    def share_wait(p, kind):
        q = (q_sib, q_across, q_other)[kind]
        part = bcp.at[quarter_rows(q), span_of(p)]
        rcopy(part, part, bs.at[p, kind], br.at[p, kind], head=h).wait_recv()

    def store_bc(p):
        span = span_of(p)
        bcp[quarter_rows(quarter), span] = res[W:W + 64].astype(BF16)
        dt[:, span] = res[W + 64:FIRST]
        share_copy(p, 0).start()
        share_copy(p, 1).start()

    def pass_bc(p):
        share_wait(p, 1)
        share_copy(p, 2).start()

    def store_x(p):
        pre[0:W, span_of(p)] = res[0:W].astype(BF16)

    def store_z(p):
        pre[W:BB, span_of(p)] = res[FIRST:FIRST + W].astype(BF16)

    pick = (lax.broadcasted_iota(jnp.int32, (16, 128), 1)
            == lax.broadcasted_iota(jnp.int32, (16, 128), 0) + 112).astype(BF16)

    def halo_copies(i):
        if i == 0:
            to, slot = jnp.where(joined, next_seq, mate), jnp.where(jnp.logical_or(ends, joined), 0, 1)
        else:
            to, slot = next_seq, 0
        yield rcopy(halo_x.at[i], in_x.at[slot], hxs.at[i], hxr.at[slot], seq=to)
        for k in range(4):
            yield rcopy(halo_b.at[i], in_b.at[slot, quarter], hbs.at[i, k], hbr.at[slot, quarter],
                        seq=to, head=base + k)

    halo_when = (jnp.logical_or(jnp.logical_not(joined), x < 3), jnp.logical_and(ends, hand_on))
    halo_slot = (order[3], 3)

    def send_halo(p):
        for i in range(2):
            @pl.when(jnp.logical_and(p == halo_slot[i], halo_when[i]))
            def _():
                tail = pl.ds(pl.multiple_of(p * 256 + 128, 128), 128)
                halo_x[i, :, 0:W] = lax.dot_general(
                    pick, pre[0:W, tail], NT, preferred_element_type=F32).astype(BF16)
                halo_b[i, :, 0:64] = lax.dot_general(
                    pick, bcp[quarter_rows(quarter), tail], NT, preferred_element_type=F32).astype(BF16)
                for copy in halo_copies(i):
                    copy.start()

    def store_first(p):
        store_bc(p)
        store_x(p)
        send_halo(p)

    def project(p, own_plane):
        complete(p, own_plane)
        product(p, 0, FIRST)
        store_first(p)

    def gates(p):
        product(p, FIRST, W)
        store_z(p)

    def taps_copy(k):
        slot = taps.at[quarter]
        return rcopy(slot, slot, cs.at[k], cr.at[quarter], head=base + (h + k + 1) % 4)

    def taps_wait(k):
        q = (h + k + 1) % 4
        rcopy(taps.at[q], taps.at[q], cs.at[k], cr.at[q], head=h).wait_recv()

    along(order[0], -1, True).start()
    along(order[0], 1, True).start()
    begin(order[0], True)
    for load in smalls + loads:
        load.start()
    for load in smalls:
        load.wait()
    taps[quarter, 0:4, 0:64] = cbc_v[...]
    for k in range(3):
        taps_copy(k).start()
    wt[W + 64:FIRST, :] = jnp.concatenate(
        [wdt_v[...].astype(F32), jnp.zeros((16 - HEADS, wt.shape[1]), F32)], axis=0).astype(BF16)
    halo_x[...] = jnp.zeros_like(halo_x)
    halo_b[...] = jnp.zeros_like(halo_b)
    for load in loads:
        load.wait()
    own.wait()

    arrive(1)
    near(order[0], True)
    arrive(2)
    last(order[0], True)
    near(order[1], False)
    project(order[0], True)
    arrive_early(2)
    near(order[2], False)
    last(order[1], False)
    arrive_early(1)
    arrive(3)
    gates(order[0])
    last(order[2], False)
    project(order[1], False)
    gates(order[1])
    near(order[3], False)
    project(order[2], False)
    pass_bc(order[0])
    arrive_early(3)
    last(order[3], False)
    pass_bc(order[1])
    pass_bc(order[2])
    complete_early(order[3])
    product(order[3], 0, FIRST, ((0, EARLY),))
    complete_late(order[3])
    product(order[3], 0, FIRST, ((EARLY, buf.shape[2] - EARLY),))
    store_first(order[3])

    def cols_of(b):
        return pl.ds(pl.multiple_of(slot_of(b // 2) * 256 + (b % 2) * 128, 128), 128)

    row = lax.broadcasted_iota(jnp.int32, (8, 128), 0)
    bias_col = jnp.zeros((8, 128), F32)
    rate_col = jnp.zeros((8, 128), F32)
    for k in range(HEADS):
        bias_col = jnp.where(row == k, bias[k], bias_col)
        rate_col = jnp.where(row == k, alog[k], rate_col)
    rate_col = jnp.exp(rate_col)
    upper = (lax.broadcasted_iota(jnp.int32, (128, 128), 0)
             <= lax.broadcasted_iota(jnp.int32, (128, 128), 1))
    parts = []
    for b in range(8):
        v = dt[0:8, cols_of(b)] + bias_col
        v = jnp.maximum(v, 0.0) + jnp.log1p(jnp.exp(-jnp.abs(v)))
        step[b * 8:(b + 1) * 8, :] = v
        parts.append(-v * rate_col)
    dec = jnp.concatenate(parts, axis=0)
    cum = jnp.dot(dec, upper.astype(F32), preferred_element_type=F32, precision=lax.Precision.HIGHEST)
    cums[...] = cum
    tot = jnp.broadcast_to(cum[:, 127:128], (64, 128))
    weight = step[...] * jnp.exp(tot - cum)
    cumt[...] = (cum - jnp.log(step[...])).T

    def mate_totals():
        return rcopy(tfin, tot_mate, ts, tr, seq=mate)

    run_t = jnp.zeros((8, 128), F32)
    first_t = run_t
    for k in range(4):
        if k:
            first_t = jnp.where(first_run == k, run_t, first_t)
            run_t = jnp.where(first_run == k, 0.0, run_t)
        for b in (2 * k, 2 * k + 1):
            offs[b] = run_t
            run_t = run_t + tot[b * 8:(b + 1) * 8, :]
    tfin[0] = jnp.where(first_run == 4, run_t, first_t)
    tfin[1] = jnp.where(first_run == 4, 0.0, run_t)
    mate_totals().start()

    lane = lax.broadcasted_iota(jnp.int32, (64, 128), 1)
    tapx = jnp.concatenate([cx_v[...], jnp.zeros((4, W), F32)], axis=0).T

    def conv_block(src, r0, taps, prev, b, dst, to):
        cur = src[r0:r0 + 64, cols_of(b)].astype(F32)
        total = taps[:, 3:4] * cur
        for k in range(1, 4):
            moved = pltpu.roll(jnp.where(lane >= 128 - k, prev, cur), k, 1)
            total = total + taps[:, 3 - k:4 - k] * moved
        dst[r0:r0 + 64, to] = silu(total).astype(BF16)
        return cur

    def conv(src, r0, taps, dst):
        prev = src[r0:r0 + 64, cols_of(0)].astype(F32)
        for b in range(1, 8):
            prev = conv_block(src, r0, taps, prev, b, dst, slice(b * 128, (b + 1) * 128))

    for k in range(HEADS):
        conv(pre, k * 64, tapx[k * 64:(k + 1) * 64], xc)
    pass_bc(order[3])
    gates(order[2])
    for k in range(3):
        taps_wait(k)
    tapb = [taps[q].T[0:64] for q in range(4)]
    for p in range(4):
        share_wait(p, 0)
        share_wait(p, 2)
    for q in range(4):
        conv(bcp, q * 64, tapb[q], bcf)

    def starts(i, b):
        to = pl.ds(pl.multiple_of(b * 128, 128), 128)
        for k in range(HEADS):
            conv_block(pre, k * 64, tapx[k * 64:(k + 1) * 64], hpad[i, k * 64:(k + 1) * 64, :], b, xc, to)
        for q in range(4):
            conv_block(bcp, q * 64, tapb[q], hpad[i, W + q * 64:W + (q + 1) * 64, :], b, bcf, to)

    halo_due = (jnp.logical_or(middle, x > 0), jnp.logical_and(ends, z != 1))
    hpad[0] = jnp.zeros((W + 256, 128), F32)
    for i in range(2):
        @pl.when(halo_due[i])
        def _():
            rcopy(halo_x.at[i], in_x.at[i], hxs.at[i], hxr.at[i], seq=s).wait_recv()
            hpad[i, 0:W, :] = lax.dot_general(in_x[i, :, 0:W], pick, TN, preferred_element_type=F32)
            for q in range(4):
                rcopy(halo_b.at[i], in_b.at[i, q], hbs.at[i, 0], hbr.at[i, q], seq=s).wait_recv()
                hpad[i, W + q * 64:W + q * 64 + 64, :] = lax.dot_general(
                    in_b[i, q, :, 0:64], pick, TN, preferred_element_type=F32)
            if i:
                starts(1, 2 * first_run)

    starts(0, 0)

    def rows(v, r):
        return jnp.concatenate(
            [jnp.broadcast_to(v[r + k:r + k + 1, :], (64, 128)) for k in range(HEADS)], axis=0)

    state = jnp.zeros((W, 128), F32)
    own_s[1] = state
    for k in range(4):
        if k:
            @pl.when(first_run == k)
            def _():
                own_s[0] = state

            state = jnp.where(first_run == k, 0.0, state)
        for b in (2 * k, 2 * k + 1):
            cols = slice(b * 128, (b + 1) * 128)
            sstart[b] = state
            xw = (xc[:, cols].astype(F32) * rows(weight, b * 8)).astype(BF16)
            fresh = lax.dot_general(xw, bcf[0:128, cols], NT, preferred_element_type=F32)
            state = state * rows(jnp.exp(tot[b * 8:(b + 1) * 8, :]), 0) + fresh

    @pl.when(first_run == 4)
    def _():
        own_s[0] = state

    @pl.when(first_run < 4)
    def _():
        own_s[1] = state

    def grown(v, t):
        return v * rows(jnp.exp(t), 0)

    mate_totals().wait_recv()
    head_t = jnp.where(ends, tfin[0], tot_mate[0])
    mid_t = jnp.where(ends, tot_mate[0], tfin[0])
    tail_t = jnp.where(ends, tfin[1], tot_mate[1])
    xfin[...] = (grown(own_s[0], jnp.where(ends, mid_t + tail_t, tail_t)) + own_s[1]).astype(BF16)
    xtot[...] = head_t + mid_t + tail_t
    for t in range(1, 4):
        @pl.when(x + t < 4)
        def _():
            rcopy(xfin, st_in.at[x], xs.at[t], xr.at[x], seq=s + 2 * t).start()
            rcopy(xtot, tot_in.at[x], vs.at[t], vr.at[x], seq=s + 2 * t).start()

    def mate_copy(i):
        return rcopy(sfin.at[i], st_mate.at[i], ss.at[i], sr.at[i], seq=mate)

    @pl.when(middle)
    def _():
        sfin[0] = own_s[0].astype(BF16)
        mate_copy(0).start()

    gates(order[3])
    inc[0] = jnp.zeros((W, 128), F32)
    for q in range(3):
        @pl.when(q < x)
        def _():
            rcopy(xfin, st_in.at[q], xs.at[0], xr.at[q], seq=s).wait_recv()
            rcopy(xtot, tot_in.at[q], vs.at[0], vr.at[q], seq=s).wait_recv()
            inc[0] = grown(inc[0], tot_in[q]) + st_in[q].astype(F32)

    carried = grown(inc[0], head_t)
    sfin[1] = jnp.where(ends, carried + own_s[0], inc[0]).astype(BF16)
    mate_copy(1).start()
    for b in range(8):
        cols = slice(b * 128, (b + 1) * 128)
        scores = lax.dot_general(bcf[0:128, cols], bcf[128:256, cols], TN, preferred_element_type=F32)
        scores = jnp.where(upper, scores, 0.0)
        for k in range(HEADS):
            r = b * 8 + k
            diff = cums[r:r + 1, :] - cumt[:, r:r + 1]
            mixing = jnp.exp(jnp.where(upper, diff, -jnp.inf)) * scores
            yin[k * 64:(k + 1) * 64, cols] = jnp.dot(
                xc[k * 64:(k + 1) * 64, cols], mixing.astype(BF16), preferred_element_type=F32)

    for k in range(3):
        taps_copy(k).wait_send()
    for j in range(4):
        p = order[j]
        for sign in (-1, 1)[:2 if j == 0 else 1 if j == 1 else 0]:
            along(p, sign, j == 0).wait_send()
            for yy in (left, right, far):
                along_early(p, yy, sign).wait_send()
        for kind in range(4):
            ring(p, kind, j == 0).wait_send()
        twin(p, y, True, j == 0).wait_send()
        for yy in (left, right, far):
            twin(p, yy, j == 0).wait_send()
            if j:
                twin_early(p, yy).wait_send()
        for kind in range(3):
            share_copy(p, kind).wait_send()

    for i in range(2):
        @pl.when(halo_when[i])
        def _():
            for copy in halo_copies(i):
                copy.wait_send()

    mate_totals().wait_send()
    mate_copy(1).wait_send()

    @pl.when(middle)
    def _():
        mate_copy(0).wait_send()

    for t in range(1, 4):
        @pl.when(x + t < 4)
        def _():
            rcopy(xfin, st_in.at[x], xs.at[t], xr.at[x], seq=s).wait_send()
            rcopy(xtot, tot_in.at[x], vs.at[t], vr.at[x], seq=s).wait_send()

    mate_copy(1).wait_recv()
    met = st_mate[1].astype(F32)
    inc[0] = jnp.where(ends, inc[0], carried) + met

    @pl.when(ends)
    def _():
        mate_copy(0).wait_recv()
        inc[1] = grown(grown(inc[0], head_t) + own_s[0], mid_t) + st_mate[0].astype(F32)

    skips = jnp.concatenate([jnp.full((64, 128), skip[k], F32) for k in range(HEADS)], axis=0)
    def send_out(dst):
        return rcopy(sb.at[dst], rbuf.at[h], as_, ar, seq=owner(dst // 8), head=dst)

    for slot in (order[3], order[1], order[2], order[0]):
        for half in range(2):
            k = (slot - turn + 4) % 4
            b = 2 * k + half
            cols = pl.ds(pl.multiple_of(b * 128, 128), 128)
            run = jnp.where(first_run <= k, 1, 0)
            st = (sstart[b] + inc[run] * rows(jnp.exp(offs[b]), 0)).astype(BF16)
            yst = jnp.dot(st, bcf[128:256, cols], preferred_element_type=F32)
            near_t = jnp.exp(cums[pl.ds(pl.multiple_of(b * 8, 8), 8), :])
            yv = yin[:, cols] + yst * rows(near_t, 0) + skips * xc[:, cols].astype(F32)
            yv = yv.astype(BF16).astype(F32)
            gate = pre[W:BB, pl.ds(pl.multiple_of(slot * 256 + half * 128, 128), 128)]
            g = (yv * silu(gate.astype(F32))).T
            for i in range(4):
                dst = slot * 8 + 4 * half + i
                sb[dst, :, 0:W] = g[32 * i:32 * i + 16, :].astype(BF16)
                sb[dst, :, W:BB] = g[32 * i + 16:32 * i + 32, :].astype(BF16)
            for i in range(4):
                dst = slot * 8 + 4 * half + i

                @pl.when(dst != h)
                def _():
                    send_out(dst).start()

    keep = pltpu.make_async_copy(sb.at[h], rbuf.at[h], lsem.at[7])
    keep.start()

    everyone = rcopy(sb.at[pl.ds(0, 31)], rbuf.at[pl.ds(0, 31)], as_, ar, head=h)
    everyone.wait_send()
    everyone.wait_recv()
    keep.wait()


def norm_kernel(parts, gain, out, held, asm, done, sems):
    loads = [pltpu.make_async_copy(parts.at[pl.ds(8 * i, 8)], held.at[pl.ds(8 * i, 8)], sems.at[i])
             for i in range(4)]
    stores = [pltpu.make_async_copy(done.at[:, pl.ds(g * 2048, 2048)], out.at[:, pl.ds(g * 2048, 2048)],
                                    sems.at[4 + g]) for g in range(5)]
    for load in loads:
        load.start()
    for i, groups in enumerate(((0,), (1,), (2,), (3, 4))):
        loads[i].wait()
        for q in range(8 * i, 8 * i + 8):
            asm[0:16, q * W:(q + 1) * W] = held[q, :, 0:W]
            asm[16:32, q * W:(q + 1) * W] = held[q, :, W:BB]
        for g in groups:
            v = asm[:, g * 2048:(g + 1) * 2048].astype(F32)
            scale = lax.rsqrt(jnp.mean(v * v, axis=1, keepdims=True) + 1e-5)
            for k in range(16):
                c0 = g * 16 + k
                done[:, c0 * 128:(c0 + 1) * 128] = (
                    v[:, k * 128:(k + 1) * 128] * scale * gain[c0:c0 + 1, :]).astype(BF16)
            stores[g].start()
    for store in stores:
        store.wait()


def call(tok, wx, wz, wbc, wdt, cx, cbc, bias, alog, skip, gain):
    d = tok.shape[1]
    anywhere = pl.BlockSpec(memory_space=pl.ANY)
    vm = pl.BlockSpec(memory_space=pltpu.VMEM)
    sm = pl.BlockSpec(memory_space=pltpu.SMEM)
    dma = pltpu.SemaphoreType.DMA
    mem = pltpu.VMEM
    parts = pl.pallas_call(
        kernel,
        out_shape=jax.ShapeDtypeStruct((32, 16, BB), BF16),
        in_specs=[anywhere] * 7 + [sm] * 3,
        out_specs=anywhere,
        scratch_shapes=[
            mem((HEADS, d), BF16), mem((4, W), F32), mem((4, 64), F32),
            mem((32, 32, d), BF16), mem((BB + 80, d), BF16), mem((BB + 80, 256), F32),
            mem((BB, 1024), BF16), mem((16, 1024), F32), mem((256, 1024), BF16), mem((256, 1024), BF16),
            mem((2, 16, 384), BF16), mem((2, 16, 128), BF16), mem((2, 16, 384), BF16), mem((2, 4, 16, 128), BF16),
            mem((2, W + 256, 128), F32), mem((4, 8, 128), F32), mem((W, 1024), BF16),
            mem((64, 128), F32), mem((64, 128), F32), mem((128, 64), F32), mem((W, 1024), F32),
            mem((8, W, 128), F32), mem((8, 8, 128), F32), mem((2, W, 128), BF16), mem((2, 8, 128), F32),
            mem((2, W, 128), BF16), mem((2, 8, 128), F32), mem((2, W, 128), F32),
            mem((W, 128), BF16), mem((8, 128), F32),
            mem((3, W, 128), BF16), mem((3, 8, 128), F32), mem((2, W, 128), F32),
            mem((32, 16, BB), BF16),
            dma((8,)), dma((4, 2)), dma((4,)), dma((4, 4, 2)), dma((4, 4)),
            dma((4, 4)), dma((4, 4)), dma((4, 4)), dma((4, 4)), dma((4, 4)), dma((4, 4)),
            dma((4, 3)), dma((4, 3)), dma((3,)), dma((4,)), dma((2,)), dma((2,)), dma((2, 4)), dma((2, 4)),
            dma((2,)), dma((2,)), dma, dma, dma((4,)), dma((3,)), dma((4,)), dma((3,)),
            dma, dma,
        ],
        compiler_params=pltpu.CompilerParams(collective_id=0, has_side_effects=True,
                                             vmem_limit_bytes=60 * 2**20),
        name="mixer",
    )(tok, wx, wz, wbc, wdt, cx, cbc, bias, alog, skip)
    return pl.pallas_call(
        norm_kernel,
        out_shape=jax.ShapeDtypeStruct((32, 10240), BF16),
        in_specs=[anywhere, vm],
        out_specs=anywhere,
        scratch_shapes=[mem((32, 16, BB), BF16), mem((32, 10240), BF16), mem((32, 10240), BF16), dma((9,))],
        name="norm",
    )(parts, gain.reshape(80, 128))


def shards(tokens, wx, wz, wbc, wdt, cx, cbc, bias, alog, skip, gain):
    return call(tokens, wx.T, wz.T, wbc.T, wdt.T, cx, cbc, bias, alog, skip, gain)


def solution(mesh):
    cols = P(None, "head")
    placed = (P(("seq", "head"), None), cols, cols, cols, cols, cols, cols,
              P("head"), P("head"), P("head"), P())
    return jax.shard_map(
        shards, mesh=mesh, in_specs=placed, out_specs=P(("seq", "head"), None), check_vma=False
    )
```
